512 devices in a mesh: space: 64 (over y, x, core), tm: 8 (over z).
Axes of the slice: x: 4, y: 8, z: 8, core: 2. Of those that a mesh axis runs over, the one named last changes fastest.
Arguments:
- dipole_rates: bfloat16 [4096, 3, 8192], P('space', None, 'tm'), may hold values from -6 to 6
- polar_rates: bfloat16 [4096, 3, 8192], P('space', None, 'tm'), may hold values from -6 to 6
- pair_counts: int32 [64, 64], P('space'), may hold values from 0 to 24, as said below
- send_blocks: int32 [64, 64, 24], P('space'), may hold values from 0 to 31, as said below
- partners: int32 [2048, 24], P('space'), may hold values from 0 to 176, as said below
Outputs:
- correlations: float32 [64, 4, 1024], P('space', None, 'tm')
The draws below stay inside these ranges and needn't reach their ends.
Inputs may be any that keep to these rules, and one draw needn't show every extreme that they name: pair_counts[e, d] is 0 unless d differs from e by 1 to 3 domains cyclically; for every sending domain e exactly one receiving domain has 24. The entries of send_blocks[e, d] are distinct block numbers of domain e; entries at or past pair_counts[e, d] are stale. `partners`: the entries of one block's list are distinct except for the empty entry 176; an entry below 32 is never the block itself.
All inputs are finite; a program needn't handle non-finite values.
Results may differ from the reference program's by a relative error of at most 0.0052.
Values may be sent and summed in bfloat16 or wider, within the bound.
No kernel may reach another device: no remote copies, remote signals or barrier semaphores. Data moves between devices by JAX's collectives and lax.ppermute only.
A program may use at most 128 MiB of HBM per device.

```python
import jax
import jax.numpy as jnp
from jax import lax

M_DEV = 64
BLK = 2
SEG = 1024
LAGS = 1024
REACH = 3
CAP = 24
SLOTS = 24
NB = 32
NIDX = 176
DOMAINS = 64
MOLECULES = 4096
BLOCKS = 2048
NT = 8192


def draw_pair_counts(key, part):
    key = jax.random.fold_in(key, 11)
    first_key, second_key = jax.random.split(key)
    sender = jnp.arange(DOMAINS, dtype=jnp.int32)[:, None]
    receiver = jnp.arange(DOMAINS, dtype=jnp.int32)[None, :]
    distance = (receiver - sender) % DOMAINS
    nearby = (distance >= 1) & (distance <= REACH) | (distance >= DOMAINS - REACH)
    values = jax.random.randint(first_key, (DOMAINS, DOMAINS), 1, CAP + 1, dtype=jnp.int32)
    chosen = jax.random.randint(second_key, (DOMAINS,), 0, 2 * REACH, dtype=jnp.int32)
    offset = jnp.where(chosen < REACH, chosen - REACH, chosen - REACH + 1)
    target = (jnp.arange(DOMAINS, dtype=jnp.int32) + offset) % DOMAINS
    values = jnp.where(receiver == target[:, None], CAP, jnp.minimum(values, CAP - 1))
    return jnp.where(nearby, values, 0).astype(jnp.int32)


def draw_send_blocks(key, part):
    key = jax.random.fold_in(key, 12)
    scores = jax.random.randint(key, (DOMAINS, DOMAINS, NB), 0, 2 ** 16, dtype=jnp.int32)
    scores = scores * NB + jnp.arange(NB, dtype=jnp.int32)
    unused, picked = lax.top_k(scores, CAP)
    return picked.astype(jnp.int32)


def draw_partners(key, part):
    key = jax.random.fold_in(key, 13)
    first_key, second_key = jax.random.split(key)
    scores = jax.random.randint(first_key, (BLOCKS, NIDX), 0, 2 ** 16, dtype=jnp.int32)
    entry = jnp.arange(NIDX, dtype=jnp.int32)
    scores = scores * NIDX + entry[None, :]
    position = jnp.arange(BLOCKS, dtype=jnp.int32) % NB
    scores = jnp.where(entry[None, :] == position[:, None], -1, scores)
    unused, picked = lax.top_k(scores, SLOTS)
    keep = jax.random.randint(second_key, (BLOCKS,), SLOTS // 2, SLOTS + 1, dtype=jnp.int32)
    keep = jnp.where(position == 0, SLOTS, jnp.where(position == 1, SLOTS // 2, keep))
    slot = jnp.arange(SLOTS, dtype=jnp.int32)[None, :]
    return jnp.where(slot < keep[:, None], picked, NIDX).astype(jnp.int32)


def levels(key, shape, cuts, least, high):
    gain = 1.0
    for dim, blocks in cuts:
        heights = jax.random.uniform(jax.random.fold_in(jax.random.fold_in(key, 6), dim), (blocks,), jnp.float32, least / len(cuts), high / len(cuts))
        gain = gain * jnp.repeat(jnp.exp(heights), shape[dim] // blocks).reshape((-1,) + (1,) * (len(shape) - 1 - dim))
    return gain


def gaussian(key, shape, spread, bound, cuts=(), held_as=jnp.bfloat16):
    array = spread * jax.random.normal(key, shape, jnp.float32)
    if cuts:
        array = array * levels(key, shape, cuts, -0.22, 0.18)
    return jnp.clip(array, -bound, bound).astype(held_as)


def setup_inputs(seed: int = 0) -> dict:
    key_of = jax.random.split(jax.random.key(seed), 6)
    return {
        "dipole_rates": gaussian(key_of[0], (MOLECULES, 3, NT), 1.0, 6.0, ((0, 64), (2, 8))),
        "polar_rates": gaussian(key_of[1], (MOLECULES, 3, NT), 1.0, 6.0, ((0, 64), (2, 8))),
        "pair_counts": draw_pair_counts(jax.random.fold_in(key_of[5], 71), 0),
        "send_blocks": draw_send_blocks(jax.random.fold_in(key_of[5], 71), 0),
        "partners": draw_partners(jax.random.fold_in(key_of[5], 71), 0),
    }


def block_totals(series):
    shaped = series.reshape(NB, BLK, 3, series.shape[2])
    return jnp.sum(shaped, axis=1, dtype=jnp.float32).astype(jnp.bfloat16)


def lag_terms(anchors, window):
    anchor_values = anchors.astype(jnp.float32)
    window_values = window.astype(jnp.float32)
    anchor_width = anchors.shape[2]
    reach_rows = window.shape[2]
    dipole_gram = jnp.einsum("bcw,bcr->wr", anchor_values, window_values[:, 0:3, :])
    polar_gram = jnp.einsum("bw,bkr->kwr", anchor_values[:, 2, :], window_values[:, 3:6, :])
    gram_stack = jnp.concatenate([dipole_gram[None], polar_gram], axis=0)
    flattened = gram_stack.reshape(4, anchor_width * reach_rows)
    flattened = jnp.pad(flattened, ((0, 0), (0, anchor_width)))
    return jnp.sum(flattened.reshape(4, anchor_width, reach_rows + 1)[:, :, :LAGS], axis=1)


def reference(dipole_rates, polar_rates, pair_counts, send_blocks, partners):
    offsets = [number - REACH for number in range(REACH)] + [number + 1 for number in range(REACH)]
    anchor_block = min(256, SEG)

    def domain_terms(domain):
        first = (domain * M_DEV).astype(jnp.int32)
        own_dipole = block_totals(lax.dynamic_slice_in_dim(dipole_rates, first, M_DEV, 0))
        own_polar = block_totals(lax.dynamic_slice_in_dim(polar_rates, first, M_DEV, 0))
        pieces = [own_dipole]
        for offset in offsets:
            source = ((domain + offset) % DOMAINS).astype(jnp.int32)
            source_dipole = block_totals(lax.dynamic_slice_in_dim(dipole_rates, (source * M_DEV).astype(jnp.int32), M_DEV, 0))
            chosen = jnp.take(source_dipole, send_blocks[source, domain], axis=0)
            live_mask = jnp.arange(CAP) < pair_counts[source, domain]
            pieces.append(jnp.where(live_mask[:, None, None], chosen, jnp.zeros_like(chosen)))
        pieces.append(jnp.zeros((1, 3, NT), jnp.bfloat16))
        shell_table = jnp.concatenate(pieces, axis=0)
        partner_rows = lax.dynamic_slice_in_dim(partners, (domain * NB).astype(jnp.int32), NB, 0)
        matches = partner_rows[:, :, None] == jnp.arange(NIDX + 1, dtype=jnp.int32)[None, None, :]
        weights = jnp.sum(matches.astype(jnp.float32), axis=1)
        shell_field = jnp.einsum("bi,ics->bcs", weights, shell_table.astype(jnp.float32)).astype(jnp.bfloat16)
        own_rates = jnp.concatenate([own_dipole, own_polar], axis=1)
        window = jnp.concatenate([own_rates, jnp.zeros((NB, 6, LAGS), jnp.bfloat16)], axis=2)

        def accumulate(block_number, totals):
            anchor_start = (block_number * anchor_block).astype(jnp.int32)
            anchors = lax.dynamic_slice_in_dim(shell_field, anchor_start, anchor_block, 2)
            rows_here = lax.dynamic_slice_in_dim(window, anchor_start, anchor_block + LAGS, 2)
            return totals + lag_terms(anchors, rows_here)

        return lax.fori_loop(0, NT // anchor_block, accumulate, jnp.zeros((4, LAGS), jnp.float32))

    raw_sums = lax.map(domain_terms, jnp.arange(DOMAINS, dtype=jnp.int32))
    anchor_count = (NT - jnp.arange(LAGS)).astype(jnp.float32)
    return raw_sums / anchor_count[None, None, :]
```

```python
import jax
import jax.numpy as jnp
from jax import lax
from jax.experimental import pallas as pl
from jax.experimental.pallas import tpu as pltpu
from jax.sharding import PartitionSpec as P

BLK = 2
LAGS = 1024
REACH = 3
LANE = 128
TILE = 256
VMEM_BYTES = 32 * 1024 * 1024


def pair_sums(rates):
    molecules = rates.shape[0]
    row = lax.broadcasted_iota(jnp.int32, (molecules // BLK, molecules), 0)
    col = lax.broadcasted_iota(jnp.int32, (molecules // BLK, molecules), 1)
    ones = ((col >= row * BLK) & (col < row * BLK + BLK)).astype(jnp.bfloat16)
    return jnp.dot(ones, rates, preferred_element_type=jnp.float32).astype(jnp.bfloat16)


def pack_kernel(domain_ref, dipole_ref, counts_ref, lists_ref, pack_ref):
    components, molecules, length = dipole_ref.shape
    blocks = molecules // BLK
    rows = components * blocks
    for c in range(components):
        totals = pair_sums(dipole_ref[c])
        for j in range(length // LANE):
            at = j * rows + c * blocks
            pack_ref[at : at + blocks, :] = totals[:, j * LANE : (j + 1) * LANE]
    capacity, domains = lists_ref.shape
    slot = lax.broadcasted_iota(jnp.int32, (16, domains), 0)
    offset = jnp.where(slot < REACH, slot - REACH, slot - REACH + 1)
    target = lax.rem(domain_ref[0] + offset + domains, domains)
    hot = (lax.broadcasted_iota(jnp.int32, (16, domains), 1) == target) & (slot < 2 * REACH)
    picked = lax.dot_general(
        hot.astype(jnp.bfloat16),
        lists_ref[...].astype(jnp.float32).astype(jnp.bfloat16),
        (((1,), (1,)), ((), ())),
        preferred_element_type=jnp.float32,
    )
    count = jnp.sum(jnp.where(hot, counts_ref[...], 0).astype(jnp.float32), axis=1, keepdims=True)
    entry = lax.broadcasted_iota(jnp.int32, (16, capacity), 1).astype(jnp.float32)
    meta = jnp.where(entry < count, picked, -1.0)
    meta = jnp.concatenate([meta, jnp.full((16, LANE - capacity), -1.0, jnp.float32)], axis=1)
    base = rows * (length // LANE)
    pack_ref[base : base + 16, :] = meta.astype(jnp.bfloat16)


def own_kernel(pack_ref, polar_ref, own_ref):
    components, molecules, length = polar_ref.shape
    blocks = molecules // BLK
    rows = components * blocks
    for j in range(length // LANE):
        own_ref[0:rows, j * LANE : (j + 1) * LANE] = pack_ref[j * rows : (j + 1) * rows, :]
    for c in range(components):
        own_ref[rows + c * blocks : rows + (c + 1) * blocks, :] = pair_sums(polar_ref[c])


def fold(gram):
    width = gram.shape[1]
    height = gram.shape[0]
    while height > LANE:
        height //= 2
        width -= height
        gram = gram[:height, :width] + gram[height:, height : height + width]
    while height > 8:
        height //= 2
        gram = gram[:height] + pltpu.roll(gram[height:], width - height, 1)
    row = lax.broadcasted_iota(jnp.int32, gram.shape, 0)
    for bit in (4, 2, 1):
        gram = jnp.where((row & bit) != 0, pltpu.roll(gram, width - bit, 1), gram)
    return jnp.sum(gram, axis=0, keepdims=True)


def sums_kernel(
    odd_ref, partners_ref, pack_ref, pa_ref, pb_ref, far_ref, spa_ref, spb_ref, sown_ref, own_ref, next_ref, out_ref, field_ref
):
    slots, blocks = partners_ref.shape
    rows = 3 * blocks
    length = own_ref.shape[1]
    odd = odd_ref[0] == 1
    capacity = slots
    received = (
        (pa_ref, 4, 1),
        (pb_ref, 1, 4),
        (far_ref, 0, 5),
        (spa_ref, 2, 3),
        (spb_ref, 5, 0),
        (sown_ref, 3, 2),
    )

    entry = lax.broadcasted_iota(jnp.int32, (blocks, blocks), 0)

    def chosen(first):
        total = jnp.zeros((blocks, blocks), jnp.float32)
        wanted = entry + first
        for s in range(slots):
            total = total + jnp.where(partners_ref[s : s + 1, :] == wanted, 1.0, 0.0)
        return total

    weights = [chosen(0).astype(jnp.bfloat16)]
    base = rows * (length // LANE)
    slot_row = lax.broadcasted_iota(jnp.int32, (16, LANE), 0)
    number = lax.broadcasted_iota(jnp.int32, (blocks, blocks), 0).astype(jnp.float32)
    for ref, at_even, at_odd in received:
        place = jnp.where(odd, at_odd, at_even)
        meta = ref[base : base + 16, :].astype(jnp.float32)
        listed = jnp.sum(jnp.where(slot_row == 2 * REACH - 1 - place, meta, 0.0), axis=0, keepdims=True)
        select = (listed[:, :blocks] == number).astype(jnp.bfloat16)
        wanted = chosen(blocks + place * capacity).astype(jnp.bfloat16)
        weights.append(jnp.dot(select, wanted, preferred_element_type=jnp.float32).astype(jnp.bfloat16))
    weight = jnp.concatenate(weights, axis=0)
    sources = [pack_ref] + [r[0] for r in received]

    for c in range(3):
        for j in range(0, length // LANE, 2):
            parts = []
            for jj in (j, j + 1):
                at = jj * rows + c * blocks
                parts.append(jnp.concatenate([ref[at : at + blocks, :] for ref in sources], axis=0))
            table = jnp.concatenate(parts, axis=1)
            field = lax.dot_general(
                weight, table, (((0,), (0,)), ((), ())), preferred_element_type=jnp.float32
            )
            field_ref[c * blocks : (c + 1) * blocks, j * LANE : (j + 2) * LANE] = field.astype(jnp.bfloat16)

    span = TILE + LAGS
    steps = length // TILE

    def later(first, count, i):
        lo = i * TILE
        here = own_ref[first : first + count, lo:length]
        return jnp.concatenate([here, next_ref[first : first + count, 0 : span - (length - lo)]], axis=1)

    def gram(anchor_first, window_first, count):
        anchors = jnp.concatenate(
            [field_ref[anchor_first : anchor_first + count, i * TILE : (i + 1) * TILE] for i in range(steps)], axis=0
        )
        window = jnp.concatenate([later(window_first, count, i) for i in range(steps)], axis=0)
        return lax.dot_general(anchors, window, (((0,), (0,)), ((), ())), preferred_element_type=jnp.float32)

    for q in range(4):
        if q == 0:
            sums = fold(gram(0, 0, rows))
        else:
            sums = fold(gram(2 * blocks, rows + (q - 1) * blocks, blocks))
        for j in range(LAGS // LANE):
            out_ref[j, q : q + 1, :] = sums[:, j * LANE : (j + 1) * LANE]


VMEM = pl.BlockSpec(memory_space=pltpu.VMEM)
SMEM = pl.BlockSpec(memory_space=pltpu.SMEM)
PARAMS = pltpu.CompilerParams(vmem_limit_bytes=VMEM_BYTES)


def per_device(dipole_rates, polar_rates, pair_counts, send_blocks, partners):
    space_size = lax.axis_size("space")
    time_size = lax.axis_size("tm")
    domain = lax.axis_index("space").astype(jnp.int32)
    molecules, components, length = dipole_rates.shape
    blocks = molecules // BLK
    rows = components * blocks
    pack_rows = rows * (length // LANE) + 16
    bf16 = jnp.bfloat16

    def moved(value, by_even, by_odd):
        pairs = [(i, (i + (by_odd if i % 2 else by_even)) % space_size) for i in range(space_size)]
        return lax.ppermute(value, "space", pairs)

    pack = pl.pallas_call(
        pack_kernel,
        out_shape=jax.ShapeDtypeStruct((pack_rows, LANE), bf16),
        in_specs=[SMEM, VMEM, VMEM, VMEM],
        out_specs=VMEM,
        compiler_params=PARAMS,
        cost_estimate=pl.CostEstimate(flops=2 * 32 * 64 * 3072, bytes_accessed=600000, transcendentals=0),
        name="pack",
    )(domain[None], dipole_rates.transpose(1, 0, 2), pair_counts, send_blocks[0].T)
    own = pl.pallas_call(
        own_kernel,
        out_shape=jax.ShapeDtypeStruct((2 * rows, length), bf16),
        in_specs=[VMEM, VMEM],
        out_specs=VMEM,
        compiler_params=PARAMS,
        cost_estimate=pl.CostEstimate(flops=2 * 32 * 64 * 3072, bytes_accessed=980000, transcendentals=0),
        name="own",
    )(pack, polar_rates.transpose(1, 0, 2))

    pa = moved(pack, -2, 2)
    pb = moved(pack, 2, -2)
    following = lax.ppermute(own, "tm", [(i, i - 1) for i in range(1, time_size)])
    sown = moved(pack, 1, -1)
    far = moved(pa, -1, 1)
    spa = moved(pa, 1, -1)
    spb = moved(pb, 1, -1)

    sums = pl.pallas_call(
        sums_kernel,
        out_shape=jax.ShapeDtypeStruct((LAGS // LANE, 4, LANE), jnp.float32),
        in_specs=[SMEM] + [VMEM] * 10,
        out_specs=VMEM,
        scratch_shapes=[pltpu.VMEM((rows, length), bf16)],
        compiler_params=PARAMS,
        cost_estimate=pl.CostEstimate(flops=2 * 300000000, bytes_accessed=2500000, transcendentals=0),
        name="sums",
    )((domain % 2)[None], partners.T, pack, pa, pb, far, spa, spb, sown, own, following)

    shares = lax.all_to_all(sums, "tm", 0, 0)
    lag_share = LAGS // time_size
    lag_index = lax.axis_index("tm") * lag_share + jnp.arange(lag_share, dtype=jnp.int32)
    anchor_count = (length * time_size - lag_index).astype(jnp.float32)
    return (jnp.sum(shares, axis=0) / anchor_count[None, :])[None]


def solution(mesh):
    return jax.shard_map(
        per_device,
        mesh=mesh,
        in_specs=(
            P("space", None, "tm"),
            P("space", None, "tm"),
            P("space", None),
            P("space", None, None),
            P("space", None),
        ),
        out_specs=P("space", None, "tm"),
        check_vma=False,
    )
```

```python
import jax
import jax.numpy as jnp
from jax import lax
from jax.experimental import pallas as pl
from jax.experimental.pallas import tpu as pltpu
from jax.sharding import PartitionSpec as P

BLK = 2
LAGS = 1024
REACH = 3
LANE = 128
TILE = 128
VMEM_BYTES = 32 * 1024 * 1024


def pair_sums(rates):
    molecules = rates.shape[0]
    row = lax.broadcasted_iota(jnp.int32, (molecules // BLK, molecules), 0)
    col = lax.broadcasted_iota(jnp.int32, (molecules // BLK, molecules), 1)
    ones = ((col >= row * BLK) & (col < row * BLK + BLK)).astype(jnp.bfloat16)
    return jnp.dot(ones, rates, preferred_element_type=jnp.float32).astype(jnp.bfloat16)


def totals_kernel(dipole_hbm, polar_hbm, own_ref, dipole_ref, polar_ref, sem):
    components, molecules, length = dipole_ref.shape
    blocks = molecules // BLK
    copies = [
        pltpu.make_async_copy(dipole_hbm, dipole_ref, sem.at[0]),
        pltpu.make_async_copy(polar_hbm, polar_ref, sem.at[1]),
    ]
    for copy in copies:
        copy.start()
    for number, (copy, ref) in enumerate(zip(copies, (dipole_ref, polar_ref))):
        copy.wait()
        for c in range(components):
            at = (number * components + c) * blocks
            own_ref[at : at + blocks, :] = pair_sums(ref[c])


def pack_kernel(domain_ref, own_ref, counts_ref, lists_ref, pack_ref):
    rows, length = own_ref.shape
    for j in range(length // LANE):
        pack_ref[j * rows : (j + 1) * rows, :] = own_ref[:, j * LANE : (j + 1) * LANE]
    capacity, domains = lists_ref.shape
    slot = lax.broadcasted_iota(jnp.int32, (16, domains), 0)
    offset = jnp.where(slot < REACH, slot - REACH, slot - REACH + 1)
    target = lax.rem(domain_ref[0] + offset + domains, domains)
    hot = (lax.broadcasted_iota(jnp.int32, (16, domains), 1) == target) & (slot < 2 * REACH)
    picked = lax.dot_general(
        hot.astype(jnp.bfloat16),
        lists_ref[...].astype(jnp.float32).astype(jnp.bfloat16),
        (((1,), (1,)), ((), ())),
        preferred_element_type=jnp.float32,
    )
    count = jnp.sum(jnp.where(hot, counts_ref[...], 0).astype(jnp.float32), axis=1, keepdims=True)
    entry = lax.broadcasted_iota(jnp.int32, (16, capacity), 1).astype(jnp.float32)
    meta = jnp.where(entry < count, picked, -1.0)
    meta = jnp.concatenate([meta, jnp.full((16, LANE - capacity), -1.0, jnp.float32)], axis=1)
    base = rows * (length // LANE)
    pack_ref[base : base + 16, :] = meta.astype(jnp.bfloat16)


def join_kernel(first_ref, second_ref, third_ref, joined_ref):
    count = first_ref.shape[0]
    for i, ref in enumerate((first_ref, second_ref, third_ref)):
        joined_ref[i * count : (i + 1) * count, :] = ref[...]


def fold(gram):
    width = gram.shape[1]
    height = gram.shape[0]
    while height > LANE:
        height //= 2
        width -= height
        gram = gram[:height, :width] + gram[height:, height : height + width]
    while height > 8:
        height //= 2
        gram = gram[:height] + pltpu.roll(gram[height:], width - height, 1)
    row = lax.broadcasted_iota(jnp.int32, gram.shape, 0)
    for bit in (4, 2, 1):
        gram = jnp.where((row & bit) != 0, pltpu.roll(gram, width - bit, 1), gram)
    return jnp.sum(gram, axis=0, keepdims=True)


def weights_of(place, meta_ref, partners_ref):
    slots, blocks = partners_ref.shape
    slot_row = lax.broadcasted_iota(jnp.int32, (16, LANE), 0)
    number = lax.broadcasted_iota(jnp.int32, (blocks, blocks), 0).astype(jnp.float32)
    meta = meta_ref[...].astype(jnp.float32)
    listed = jnp.sum(jnp.where(slot_row == 2 * REACH - 1 - place, meta, 0.0), axis=0, keepdims=True)
    select = (listed[:, :blocks] == number).astype(jnp.bfloat16)
    wanted = named_by(blocks + place * slots, partners_ref).astype(jnp.bfloat16)
    return jnp.dot(select, wanted, preferred_element_type=jnp.float32).astype(jnp.bfloat16)


def named_by(first, partners_ref):
    slots, blocks = partners_ref.shape
    wanted = lax.broadcasted_iota(jnp.int32, (blocks, blocks), 0) + first
    total = jnp.zeros((blocks, blocks), jnp.float32)
    for s in range(slots):
        total = total + jnp.where(partners_ref[s : s + 1, :] == wanted, 1.0, 0.0)
    return total


def field_terms(weight, sources, blocks, length, store):
    rows = 3 * blocks
    for c in range(3):
        for j in range(0, length // LANE, 2):
            parts = []
            for jj in (j, j + 1):
                at = jj * rows + c * blocks
                parts.append(jnp.concatenate([ref[at : at + blocks, :] for ref in sources], axis=0))
            table = jnp.concatenate(parts, axis=1)
            field = lax.dot_general(
                weight, table, (((0,), (0,)), ((), ())), preferred_element_type=jnp.float32
            )
            store(slice(c * blocks, (c + 1) * blocks), slice(j * LANE, (j + 2) * LANE), field)


def near_kernel(odd_ref, partners_ref, pack_ref, pa_ref, pb_ref, part_ref):
    slots, blocks = partners_ref.shape
    rows, length = part_ref.shape
    base = rows * (length // LANE)
    odd = odd_ref[0] == 1
    weights = [named_by(0, partners_ref).astype(jnp.bfloat16)]
    for ref, at_even, at_odd in ((pa_ref, 4, 1), (pb_ref, 1, 4)):
        weights.append(weights_of(jnp.where(odd, at_odd, at_even), ref.at[pl.ds(base, 16)], partners_ref))

    def store(row, col, field):
        part_ref[row, col] = field

    field_terms(jnp.concatenate(weights, axis=0), [pack_ref, pa_ref, pb_ref], blocks, length, store)


def sums_kernel(odd_ref, partners_ref, part_ref, far_ref, swap_ref, own_ref, next_ref, out_ref, field_ref):
    slots, blocks = partners_ref.shape
    rows = 3 * blocks
    length = own_ref.shape[1]
    base = rows * (length // LANE)
    odd = odd_ref[0] == 1
    count = far_ref.shape[0]
    sown_ref, spa_ref, spb_ref = [swap_ref.at[pl.ds(i * count, count)] for i in range(3)]
    weights = []
    for ref, at_even, at_odd in ((far_ref, 0, 5), (spa_ref, 2, 3), (spb_ref, 5, 0), (sown_ref, 3, 2)):
        weights.append(weights_of(jnp.where(odd, at_odd, at_even), ref.at[pl.ds(base, 16)], partners_ref))

    def store(row, col, field):
        field_ref[row, col] = (part_ref[row, col] + field).astype(jnp.bfloat16)

    field_terms(jnp.concatenate(weights, axis=0), [far_ref, spa_ref, spb_ref, sown_ref], blocks, length, store)

    span = TILE + LAGS
    steps = length // TILE

    def later(first, count, i):
        lo = i * TILE
        here = own_ref[first : first + count, lo:length]
        return jnp.concatenate([here, next_ref[first : first + count, 0 : span - (length - lo)]], axis=1)

    def gram(anchor_first, window_first, count):
        anchors = jnp.concatenate(
            [field_ref[anchor_first : anchor_first + count, i * TILE : (i + 1) * TILE] for i in range(steps)], axis=0
        )
        window = jnp.concatenate([later(window_first, count, i) for i in range(steps)], axis=0)
        return lax.dot_general(anchors, window, (((0,), (0,)), ((), ())), preferred_element_type=jnp.float32)

    for q in range(4):
        if q == 0:
            sums = fold(gram(0, 0, rows))
        else:
            sums = fold(gram(2 * blocks, rows + (q - 1) * blocks, blocks))
        for j in range(LAGS // LANE):
            out_ref[j, q : q + 1, :] = sums[:, j * LANE : (j + 1) * LANE]


VMEM = pl.BlockSpec(memory_space=pltpu.VMEM)
HBM = pl.BlockSpec(memory_space=pltpu.HBM)
SMEM = pl.BlockSpec(memory_space=pltpu.SMEM)
TOTALS_PARAMS = pltpu.CompilerParams(vmem_limit_bytes=54784 * 1024)
PARAMS = pltpu.CompilerParams(vmem_limit_bytes=VMEM_BYTES)


def per_device(dipole_rates, polar_rates, pair_counts, send_blocks, partners):
    space_size = lax.axis_size("space")
    time_size = lax.axis_size("tm")
    domain = lax.axis_index("space").astype(jnp.int32)
    molecules, components, length = dipole_rates.shape
    blocks = molecules // BLK
    rows = components * blocks
    pack_rows = rows * (length // LANE) + 16
    bf16 = jnp.bfloat16

    def moved(value, by_even, by_odd):
        pairs = [(i, (i + (by_odd if i % 2 else by_even)) % space_size) for i in range(space_size)]
        return lax.ppermute(value, "space", pairs)

    own = pl.pallas_call(
        totals_kernel,
        out_shape=jax.ShapeDtypeStruct((2 * rows, length), bf16),
        in_specs=[HBM, HBM],
        out_specs=VMEM,
        scratch_shapes=[
            pltpu.VMEM((components, molecules, length), bf16),
            pltpu.VMEM((components, molecules, length), bf16),
            pltpu.SemaphoreType.DMA((2,)),
        ],
        compiler_params=TOTALS_PARAMS,
        cost_estimate=pl.CostEstimate(flops=4 * 32 * 64 * 3072, bytes_accessed=1200000, transcendentals=0),
        name="totals",
    )(dipole_rates.transpose(1, 0, 2), polar_rates.transpose(1, 0, 2))
    pack = pl.pallas_call(
        pack_kernel,
        out_shape=jax.ShapeDtypeStruct((pack_rows, LANE), bf16),
        grid=(1,),
        in_specs=[
            SMEM,
            pl.BlockSpec((rows, length), lambda i: (0, 0)),
            pl.BlockSpec((1, space_size), lambda i: (0, 0)),
            pl.BlockSpec((send_blocks.shape[2], space_size), lambda i: (0, 0)),
        ],
        out_specs=pl.BlockSpec((pack_rows, LANE), lambda i: (0, 0)),
        compiler_params=PARAMS,
        cost_estimate=pl.CostEstimate(flops=10**10, bytes_accessed=400000, transcendentals=0),
        name="pack",
    )(domain[None], own, pair_counts, send_blocks[0].T)

    following = lax.ppermute(own, "tm", [(i, i - 1) for i in range(1, time_size)])
    pa = moved(pack, -2, 2)
    pb = moved(pack, 2, -2)
    far = moved(pack, -3, 3)
    joined = pl.pallas_call(
        join_kernel,
        out_shape=jax.ShapeDtypeStruct((3 * pack_rows, LANE), bf16),
        in_specs=[VMEM] * 3,
        out_specs=VMEM,
        compiler_params=PARAMS,
        cost_estimate=pl.CostEstimate(flops=0, bytes_accessed=1200000, transcendentals=0),
        name="join",
    )(pack, pa, pb)
    swapped = moved(joined, 1, -1)

    odd = (domain % 2)[None]
    pa_later, following = lax.optimization_barrier((pa, following))
    part = pl.pallas_call(
        near_kernel,
        out_shape=jax.ShapeDtypeStruct((rows, length), jnp.float32),
        in_specs=[SMEM] + [VMEM] * 4,
        out_specs=VMEM,
        compiler_params=PARAMS,
        cost_estimate=pl.CostEstimate(flops=10**10, bytes_accessed=1000000, transcendentals=0),
        name="near",
    )(odd, partners.T, pack, pa_later, pb)
    sums = pl.pallas_call(
        sums_kernel,
        out_shape=jax.ShapeDtypeStruct((LAGS // LANE, 4, LANE), jnp.float32),
        in_specs=[SMEM] + [VMEM] * 6,
        out_specs=VMEM,
        scratch_shapes=[pltpu.VMEM((rows, length), bf16)],
        compiler_params=PARAMS,
        cost_estimate=pl.CostEstimate(flops=2 * 300000000, bytes_accessed=2500000, transcendentals=0),
        name="sums",
    )(odd, partners.T, part, far, swapped, own, following)

    shares = lax.all_to_all(sums, "tm", 0, 0)
    lag_share = LAGS // time_size
    lag_index = lax.axis_index("tm") * lag_share + jnp.arange(lag_share, dtype=jnp.int32)
    anchor_count = (length * time_size - lag_index).astype(jnp.float32)
    return (jnp.sum(shares, axis=0) / anchor_count[None, :])[None]


def solution(mesh):
    return jax.shard_map(
        per_device,
        mesh=mesh,
        in_specs=(
            P("space", None, "tm"),
            P("space", None, "tm"),
            P("space", None),
            P("space", None, None),
            P("space", None),
        ),
        out_specs=P("space", None, "tm"),
        check_vma=False,
    )
```

```python
import jax
import jax.numpy as jnp
from jax import lax
from jax.experimental import pallas as pl
from jax.experimental.pallas import tpu as pltpu
from jax.sharding import PartitionSpec as P

BLK = 2
LAGS = 1024
REACH = 3
LANE = 128
TILE = 128
VMEM_BYTES = 32 * 1024 * 1024


def pair_sums(rates):
    molecules = rates.shape[0]
    row = lax.broadcasted_iota(jnp.int32, (molecules // BLK, molecules), 0)
    col = lax.broadcasted_iota(jnp.int32, (molecules // BLK, molecules), 1)
    ones = ((col >= row * BLK) & (col < row * BLK + BLK)).astype(jnp.bfloat16)
    return jnp.dot(ones, rates, preferred_element_type=jnp.float32).astype(jnp.bfloat16)


def totals_kernel(dipole_hbm, polar_hbm, own_ref, dipole_ref, polar_ref, sem):
    components, molecules, length = dipole_ref.shape
    blocks = molecules // BLK
    copies = [
        pltpu.make_async_copy(dipole_hbm, dipole_ref, sem.at[0]),
        pltpu.make_async_copy(polar_hbm, polar_ref, sem.at[1]),
    ]
    for copy in copies:
        copy.start()
    for number, (copy, ref) in enumerate(zip(copies, (dipole_ref, polar_ref))):
        copy.wait()
        for c in range(components):
            at = (number * components + c) * blocks
            own_ref[at : at + blocks, :] = pair_sums(ref[c])


def pack_kernel(domain_ref, own_ref, counts_ref, lists_ref, pack_ref):
    rows, length = own_ref.shape
    for j in range(length // LANE):
        pack_ref[j * rows : (j + 1) * rows, :] = own_ref[:, j * LANE : (j + 1) * LANE]
    capacity, domains = lists_ref.shape
    slot = lax.broadcasted_iota(jnp.int32, (16, domains), 0)
    offset = jnp.where(slot < REACH, slot - REACH, slot - REACH + 1)
    target = lax.rem(domain_ref[0] + offset + domains, domains)
    hot = (lax.broadcasted_iota(jnp.int32, (16, domains), 1) == target) & (slot < 2 * REACH)
    picked = lax.dot_general(
        hot.astype(jnp.bfloat16),
        lists_ref[...].astype(jnp.float32).astype(jnp.bfloat16),
        (((1,), (1,)), ((), ())),
        preferred_element_type=jnp.float32,
    )
    count = jnp.sum(jnp.where(hot, counts_ref[...], 0).astype(jnp.float32), axis=1, keepdims=True)
    entry = lax.broadcasted_iota(jnp.int32, (16, capacity), 1).astype(jnp.float32)
    meta = jnp.where(entry < count, picked, -1.0)
    meta = jnp.concatenate([meta, jnp.full((16, LANE - capacity), -1.0, jnp.float32)], axis=1)
    base = rows * (length // LANE)
    pack_ref[base : base + 16, :] = meta.astype(jnp.bfloat16)


def touch_kernel(a_ref, b_ref):
    b_ref[...] = a_ref[...]


def join_kernel(first_ref, second_ref, third_ref, joined_ref):
    count = first_ref.shape[0]
    for i, ref in enumerate((first_ref, second_ref, third_ref)):
        joined_ref[i * count : (i + 1) * count, :] = ref[...]


def fold(gram):
    width = gram.shape[1]
    height = gram.shape[0]
    while height > LANE:
        height //= 2
        width -= height
        gram = gram[:height, :width] + gram[height:, height : height + width]
    while height > 8:
        height //= 2
        gram = gram[:height] + pltpu.roll(gram[height:], width - height, 1)
    row = lax.broadcasted_iota(jnp.int32, gram.shape, 0)
    for bit in (4, 2, 1):
        gram = jnp.where((row & bit) != 0, pltpu.roll(gram, width - bit, 1), gram)
    return jnp.sum(gram, axis=0, keepdims=True)


def weights_of(place, meta_ref, partners_ref):
    slots, blocks = partners_ref.shape
    slot_row = lax.broadcasted_iota(jnp.int32, (16, LANE), 0)
    number = lax.broadcasted_iota(jnp.int32, (blocks, blocks), 0).astype(jnp.float32)
    meta = meta_ref[...].astype(jnp.float32)
    listed = jnp.sum(jnp.where(slot_row == 2 * REACH - 1 - place, meta, 0.0), axis=0, keepdims=True)
    select = (listed[:, :blocks] == number).astype(jnp.bfloat16)
    wanted = named_by(blocks + place * slots, partners_ref).astype(jnp.bfloat16)
    return jnp.dot(select, wanted, preferred_element_type=jnp.float32).astype(jnp.bfloat16)


def named_by(first, partners_ref):
    slots, blocks = partners_ref.shape
    wanted = lax.broadcasted_iota(jnp.int32, (blocks, blocks), 0) + first
    total = jnp.zeros((blocks, blocks), jnp.float32)
    for s in range(slots):
        total = total + jnp.where(partners_ref[s : s + 1, :] == wanted, 1.0, 0.0)
    return total


def field_terms(weight, sources, blocks, length, store):
    rows = 3 * blocks
    for c in range(3):
        for j in range(0, length // LANE, 2):
            parts = []
            for jj in (j, j + 1):
                at = jj * rows + c * blocks
                parts.append(jnp.concatenate([ref[at : at + blocks, :] for ref in sources], axis=0))
            table = jnp.concatenate(parts, axis=1)
            field = lax.dot_general(
                weight, table, (((0,), (0,)), ((), ())), preferred_element_type=jnp.float32
            )
            store(slice(c * blocks, (c + 1) * blocks), slice(j * LANE, (j + 2) * LANE), field)


def near_kernel(odd_ref, partners_ref, pack_ref, pa_ref, pb_ref, part_ref):
    slots, blocks = partners_ref.shape
    rows, length = part_ref.shape
    base = rows * (length // LANE)
    odd = odd_ref[0] == 1
    weights = [named_by(0, partners_ref).astype(jnp.bfloat16)]
    for ref, at_even, at_odd in ((pa_ref, 4, 1), (pb_ref, 1, 4)):
        weights.append(weights_of(jnp.where(odd, at_odd, at_even), ref.at[pl.ds(base, 16)], partners_ref))

    def store(row, col, field):
        part_ref[row, col] = field

    field_terms(jnp.concatenate(weights, axis=0), [pack_ref, pa_ref, pb_ref], blocks, length, store)


def sums_kernel(odd_ref, partners_ref, part_ref, far_ref, swap_ref, own_ref, next_ref, out_ref, field_ref):
    slots, blocks = partners_ref.shape
    rows = 3 * blocks
    length = own_ref.shape[1]
    base = rows * (length // LANE)
    odd = odd_ref[0] == 1
    count = far_ref.shape[0]
    sown_ref, spa_ref, spb_ref = [swap_ref.at[pl.ds(i * count, count)] for i in range(3)]
    weights = []
    for ref, at_even, at_odd in ((far_ref, 0, 5), (spa_ref, 2, 3), (spb_ref, 5, 0), (sown_ref, 3, 2)):
        weights.append(weights_of(jnp.where(odd, at_odd, at_even), ref.at[pl.ds(base, 16)], partners_ref))

    def store(row, col, field):
        field_ref[row, col] = (part_ref[row, col] + field).astype(jnp.bfloat16)

    field_terms(jnp.concatenate(weights, axis=0), [far_ref, spa_ref, spb_ref, sown_ref], blocks, length, store)

    span = TILE + LAGS
    steps = length // TILE

    def later(first, count, i):
        lo = i * TILE
        here = own_ref[first : first + count, lo:length]
        return jnp.concatenate([here, next_ref[first : first + count, 0 : span - (length - lo)]], axis=1)

    def gram(anchor_first, window_first, count):
        anchors = jnp.concatenate(
            [field_ref[anchor_first : anchor_first + count, i * TILE : (i + 1) * TILE] for i in range(steps)], axis=0
        )
        window = jnp.concatenate([later(window_first, count, i) for i in range(steps)], axis=0)
        return lax.dot_general(anchors, window, (((0,), (0,)), ((), ())), preferred_element_type=jnp.float32)

    for q in range(4):
        if q == 0:
            sums = fold(gram(0, 0, rows))
        else:
            sums = fold(gram(2 * blocks, rows + (q - 1) * blocks, blocks))
        for j in range(LAGS // LANE):
            out_ref[j, q : q + 1, :] = sums[:, j * LANE : (j + 1) * LANE]


VMEM = pl.BlockSpec(memory_space=pltpu.VMEM)
HBM = pl.BlockSpec(memory_space=pltpu.HBM)
SMEM = pl.BlockSpec(memory_space=pltpu.SMEM)
TOTALS_PARAMS = pltpu.CompilerParams(vmem_limit_bytes=54784 * 1024)
PARAMS = pltpu.CompilerParams(vmem_limit_bytes=VMEM_BYTES)


def per_device(dipole_rates, polar_rates, pair_counts, send_blocks, partners):
    space_size = lax.axis_size("space")
    time_size = lax.axis_size("tm")
    domain = lax.axis_index("space").astype(jnp.int32)
    molecules, components, length = dipole_rates.shape
    blocks = molecules // BLK
    rows = components * blocks
    pack_rows = rows * (length // LANE) + 16
    bf16 = jnp.bfloat16

    def moved(value, by_even, by_odd):
        pairs = [(i, (i + (by_odd if i % 2 else by_even)) % space_size) for i in range(space_size)]
        return lax.ppermute(value, "space", pairs)

    own = pl.pallas_call(
        totals_kernel,
        out_shape=jax.ShapeDtypeStruct((2 * rows, length), bf16),
        in_specs=[HBM, HBM],
        out_specs=VMEM,
        scratch_shapes=[
            pltpu.VMEM((components, molecules, length), bf16),
            pltpu.VMEM((components, molecules, length), bf16),
            pltpu.SemaphoreType.DMA((2,)),
        ],
        compiler_params=TOTALS_PARAMS,
        cost_estimate=pl.CostEstimate(flops=4 * 32 * 64 * 3072, bytes_accessed=1200000, transcendentals=0),
        name="totals",
    )(dipole_rates.transpose(1, 0, 2), polar_rates.transpose(1, 0, 2))
    pack = pl.pallas_call(
        pack_kernel,
        out_shape=jax.ShapeDtypeStruct((pack_rows, LANE), bf16),
        grid=(1,),
        in_specs=[
            SMEM,
            pl.BlockSpec((rows, length), lambda i: (0, 0)),
            pl.BlockSpec((1, space_size), lambda i: (0, 0)),
            pl.BlockSpec((send_blocks.shape[2], space_size), lambda i: (0, 0)),
        ],
        out_specs=pl.BlockSpec((pack_rows, LANE), lambda i: (0, 0)),
        compiler_params=PARAMS,
        cost_estimate=pl.CostEstimate(flops=10**6, bytes_accessed=400000, transcendentals=0),
        name="pack",
    )(domain[None], own, pair_counts, send_blocks[0].T)

    following = lax.ppermute(own, "tm", [(i, i - 1) for i in range(1, time_size)])
    pa = moved(pack, -2, 2)
    pb = moved(pack, 2, -2)
    far_pack = pl.pallas_call(
        touch_kernel,
        out_shape=jax.ShapeDtypeStruct((pack_rows, LANE), bf16),
        in_specs=[VMEM],
        out_specs=VMEM,
        compiler_params=PARAMS,
        cost_estimate=pl.CostEstimate(flops=10**6, bytes_accessed=400000, transcendentals=0),
        name="touch",
    )(pack)
    far = moved(far_pack, -3, 3)
    joined = pl.pallas_call(
        join_kernel,
        out_shape=jax.ShapeDtypeStruct((3 * pack_rows, LANE), bf16),
        in_specs=[VMEM] * 3,
        out_specs=VMEM,
        compiler_params=PARAMS,
        cost_estimate=pl.CostEstimate(flops=3*10**9, bytes_accessed=1200000, transcendentals=0),
        name="join",
    )(pack, pa, pb)
    swapped = moved(joined, 1, -1)

    odd = (domain % 2)[None]
    pa_later, following = lax.optimization_barrier((pa, following))
    part = pl.pallas_call(
        near_kernel,
        out_shape=jax.ShapeDtypeStruct((rows, length), jnp.float32),
        in_specs=[SMEM] + [VMEM] * 4,
        out_specs=VMEM,
        compiler_params=PARAMS,
        cost_estimate=pl.CostEstimate(flops=10**10, bytes_accessed=1000000, transcendentals=0),
        name="near",
    )(odd, partners.T, pack, pa_later, pb)
    sums = pl.pallas_call(
        sums_kernel,
        out_shape=jax.ShapeDtypeStruct((LAGS // LANE, 4, LANE), jnp.float32),
        in_specs=[SMEM] + [VMEM] * 6,
        out_specs=VMEM,
        scratch_shapes=[pltpu.VMEM((rows, length), bf16)],
        compiler_params=PARAMS,
        cost_estimate=pl.CostEstimate(flops=2 * 300000000, bytes_accessed=2500000, transcendentals=0),
        name="sums",
    )(odd, partners.T, part, far, swapped, own, following)

    shares = lax.all_to_all(sums, "tm", 0, 0)
    lag_share = LAGS // time_size
    lag_index = lax.axis_index("tm") * lag_share + jnp.arange(lag_share, dtype=jnp.int32)
    anchor_count = (length * time_size - lag_index).astype(jnp.float32)
    return (jnp.sum(shares, axis=0) / anchor_count[None, :])[None]


def solution(mesh):
    return jax.shard_map(
        per_device,
        mesh=mesh,
        in_specs=(
            P("space", None, "tm"),
            P("space", None, "tm"),
            P("space", None),
            P("space", None, None),
            P("space", None),
        ),
        out_specs=P("space", None, "tm"),
        check_vma=False,
    )
```

```python
import jax
import jax.numpy as jnp
from jax import lax
from jax.experimental import pallas as pl
from jax.experimental.pallas import tpu as pltpu
from jax.sharding import PartitionSpec as P

BLK = 2
LAGS = 1024
REACH = 3
LANE = 128
TILE = 128
VMEM_BYTES = 32 * 1024 * 1024


def pair_sums(rates):
    molecules = rates.shape[0]
    row = lax.broadcasted_iota(jnp.int32, (molecules // BLK, molecules), 0)
    col = lax.broadcasted_iota(jnp.int32, (molecules // BLK, molecules), 1)
    ones = ((col >= row * BLK) & (col < row * BLK + BLK)).astype(jnp.bfloat16)
    return jnp.dot(ones, rates, preferred_element_type=jnp.float32).astype(jnp.bfloat16)


def totals_kernel(dipole_hbm, polar_hbm, own_ref, dipole_ref, polar_ref, sem):
    components, molecules, length = dipole_ref.shape
    blocks = molecules // BLK
    copies = [
        pltpu.make_async_copy(dipole_hbm, dipole_ref, sem.at[0]),
        pltpu.make_async_copy(polar_hbm, polar_ref, sem.at[1]),
    ]
    for copy in copies:
        copy.start()
    for number, (copy, ref) in enumerate(zip(copies, (dipole_ref, polar_ref))):
        copy.wait()
        for c in range(components):
            at = (number * components + c) * blocks
            own_ref[at : at + blocks, :] = pair_sums(ref[c])


def pack_kernel(domain_ref, own_ref, counts_ref, lists_ref, pack_ref):
    rows, length = own_ref.shape
    for j in range(length // LANE):
        pack_ref[j * rows : (j + 1) * rows, :] = own_ref[:, j * LANE : (j + 1) * LANE]
    capacity, domains = lists_ref.shape
    slot = lax.broadcasted_iota(jnp.int32, (16, domains), 0)
    offset = jnp.where(slot < REACH, slot - REACH, slot - REACH + 1)
    target = lax.rem(domain_ref[0] + offset + domains, domains)
    hot = (lax.broadcasted_iota(jnp.int32, (16, domains), 1) == target) & (slot < 2 * REACH)
    picked = lax.dot_general(
        hot.astype(jnp.bfloat16),
        lists_ref[...].astype(jnp.float32).astype(jnp.bfloat16),
        (((1,), (1,)), ((), ())),
        preferred_element_type=jnp.float32,
    )
    count = jnp.sum(jnp.where(hot, counts_ref[...], 0).astype(jnp.float32), axis=1, keepdims=True)
    entry = lax.broadcasted_iota(jnp.int32, (16, capacity), 1).astype(jnp.float32)
    meta = jnp.where(entry < count, picked, -1.0)
    meta = jnp.concatenate([meta, jnp.full((16, LANE - capacity), -1.0, jnp.float32)], axis=1)
    base = rows * (length // LANE)
    pack_ref[base : base + 16, :] = meta.astype(jnp.bfloat16)


def touch_kernel(a_ref, unused_ref, b_ref):
    b_ref[...] = a_ref[...]


def fold(gram):
    width = gram.shape[1]
    height = gram.shape[0]
    while height > LANE:
        height //= 2
        width -= height
        gram = gram[:height, :width] + gram[height:, height : height + width]
    while height > 8:
        height //= 2
        gram = gram[:height] + pltpu.roll(gram[height:], width - height, 1)
    row = lax.broadcasted_iota(jnp.int32, gram.shape, 0)
    for bit in (4, 2, 1):
        gram = jnp.where((row & bit) != 0, pltpu.roll(gram, width - bit, 1), gram)
    return jnp.sum(gram, axis=0, keepdims=True)


def weights_of(place, meta_ref, partners_ref):
    slots, blocks = partners_ref.shape
    slot_row = lax.broadcasted_iota(jnp.int32, (16, LANE), 0)
    number = lax.broadcasted_iota(jnp.int32, (blocks, blocks), 0).astype(jnp.float32)
    meta = meta_ref[...].astype(jnp.float32)
    listed = jnp.sum(jnp.where(slot_row == 2 * REACH - 1 - place, meta, 0.0), axis=0, keepdims=True)
    select = (listed[:, :blocks] == number).astype(jnp.bfloat16)
    wanted = named_by(blocks + place * slots, partners_ref).astype(jnp.bfloat16)
    return jnp.dot(select, wanted, preferred_element_type=jnp.float32).astype(jnp.bfloat16)


def named_by(first, partners_ref):
    slots, blocks = partners_ref.shape
    wanted = lax.broadcasted_iota(jnp.int32, (blocks, blocks), 0) + first
    total = jnp.zeros((blocks, blocks), jnp.float32)
    for s in range(slots):
        total = total + jnp.where(partners_ref[s : s + 1, :] == wanted, 1.0, 0.0)
    return total


def field_terms(weight, sources, blocks, length, store):
    rows = 3 * blocks
    for c in range(3):
        for j in range(0, length // LANE, 2):
            parts = []
            for jj in (j, j + 1):
                at = jj * rows + c * blocks
                parts.append(jnp.concatenate([ref[at : at + blocks, :] for ref in sources], axis=0))
            table = jnp.concatenate(parts, axis=1)
            field = lax.dot_general(
                weight, table, (((0,), (0,)), ((), ())), preferred_element_type=jnp.float32
            )
            store(slice(c * blocks, (c + 1) * blocks), slice(j * LANE, (j + 2) * LANE), field)


def near_kernel(odd_ref, partners_ref, both_ref, side_ref, part_ref):
    slots, blocks = partners_ref.shape
    rows, length = part_ref.shape
    base = rows * (length // LANE)
    count = base + 16
    odd = odd_ref[0] == 1
    mine = named_by(0, partners_ref).astype(jnp.bfloat16)
    refs = [both_ref.at[pl.ds(0, count)], both_ref.at[pl.ds(count, count)]]
    refs += [side_ref.at[pl.ds(0, count)], side_ref.at[pl.ds(count, count)]]
    weights = [
        jnp.where(odd, weights_of(2, refs[0].at[pl.ds(base, 16)], partners_ref), mine),
        jnp.where(odd, mine, weights_of(3, refs[1].at[pl.ds(base, 16)], partners_ref)),
    ]
    for ref, at_even, at_odd in ((refs[2], 1, 3), (refs[3], 2, 4)):
        weights.append(weights_of(jnp.where(odd, at_odd, at_even), ref.at[pl.ds(base, 16)], partners_ref))

    def store(row, col, field):
        part_ref[row, col] = field

    field_terms(jnp.concatenate(weights, axis=0), refs, blocks, length, store)


def sums_kernel(odd_ref, partners_ref, part_ref, far_ref, swap_ref, own_ref, next_ref, out_ref, field_ref):
    slots, blocks = partners_ref.shape
    rows = 3 * blocks
    length = own_ref.shape[1]
    base = rows * (length // LANE)
    odd = odd_ref[0] == 1
    count = far_ref.shape[0]
    refs = [far_ref, swap_ref.at[pl.ds(0, count)], swap_ref.at[pl.ds(count, count)]]
    weights = []
    for ref, at_even, at_odd in zip(refs, (0, 4, 5), (5, 0, 1)):
        weights.append(weights_of(jnp.where(odd, at_odd, at_even), ref.at[pl.ds(base, 16)], partners_ref))

    def store(row, col, field):
        field_ref[row, col] = (part_ref[row, col] + field).astype(jnp.bfloat16)

    field_terms(jnp.concatenate(weights, axis=0), refs, blocks, length, store)

    span = TILE + LAGS
    steps = length // TILE

    def later(first, count, i):
        lo = i * TILE
        here = own_ref[first : first + count, lo:length]
        return jnp.concatenate([here, next_ref[first : first + count, 0 : span - (length - lo)]], axis=1)

    def gram(anchor_first, window_first, count):
        anchors = jnp.concatenate(
            [field_ref[anchor_first : anchor_first + count, i * TILE : (i + 1) * TILE] for i in range(steps)], axis=0
        )
        window = jnp.concatenate([later(window_first, count, i) for i in range(steps)], axis=0)
        return lax.dot_general(anchors, window, (((0,), (0,)), ((), ())), preferred_element_type=jnp.float32)

    for q in range(4):
        if q == 0:
            sums = fold(gram(0, 0, rows))
        else:
            sums = fold(gram(2 * blocks, rows + (q - 1) * blocks, blocks))
        for j in range(LAGS // LANE):
            out_ref[j, q : q + 1, :] = sums[:, j * LANE : (j + 1) * LANE]


VMEM = pl.BlockSpec(memory_space=pltpu.VMEM)
HBM = pl.BlockSpec(memory_space=pltpu.HBM)
SMEM = pl.BlockSpec(memory_space=pltpu.SMEM)
TOTALS_PARAMS = pltpu.CompilerParams(vmem_limit_bytes=54784 * 1024)
PARAMS = pltpu.CompilerParams(vmem_limit_bytes=VMEM_BYTES)


def per_device(dipole_rates, polar_rates, pair_counts, send_blocks, partners):
    space_size = lax.axis_size("space")
    time_size = lax.axis_size("tm")
    domain = lax.axis_index("space").astype(jnp.int32)
    molecules, components, length = dipole_rates.shape
    blocks = molecules // BLK
    rows = components * blocks
    pack_rows = rows * (length // LANE) + 16
    bf16 = jnp.bfloat16

    def moved(value, by_even, by_odd):
        pairs = [(i, (i + (by_odd if i % 2 else by_even)) % space_size) for i in range(space_size)]
        return lax.ppermute(value, "space", pairs)

    own = pl.pallas_call(
        totals_kernel,
        out_shape=jax.ShapeDtypeStruct((2 * rows, length), bf16),
        in_specs=[HBM, HBM],
        out_specs=VMEM,
        scratch_shapes=[
            pltpu.VMEM((components, molecules, length), bf16),
            pltpu.VMEM((components, molecules, length), bf16),
            pltpu.SemaphoreType.DMA((2,)),
        ],
        compiler_params=TOTALS_PARAMS,
        cost_estimate=pl.CostEstimate(flops=4 * 32 * 64 * 3072, bytes_accessed=1200000, transcendentals=0),
        name="totals",
    )(dipole_rates.transpose(1, 0, 2), polar_rates.transpose(1, 0, 2))
    pack = pl.pallas_call(
        pack_kernel,
        out_shape=jax.ShapeDtypeStruct((pack_rows, LANE), bf16),
        grid=(1,),
        in_specs=[
            SMEM,
            pl.BlockSpec((rows, length), lambda i: (0, 0)),
            pl.BlockSpec((1, space_size), lambda i: (0, 0)),
            pl.BlockSpec((send_blocks.shape[2], space_size), lambda i: (0, 0)),
        ],
        out_specs=pl.BlockSpec((pack_rows, LANE), lambda i: (0, 0)),
        compiler_params=PARAMS,
        cost_estimate=pl.CostEstimate(flops=10**6, bytes_accessed=400000, transcendentals=0),
        name="pack",
    )(domain[None], own, pair_counts, send_blocks[0].T)

    pairs = [[2 * i, 2 * i + 1] for i in range(space_size // 2)]
    both = lax.all_gather(pack, "space", axis_index_groups=pairs, tiled=True)
    own_later = own
    side = moved(both, -1, 1)
    following = lax.ppermute(own_later, "tm", [(i, i - 1) for i in range(1, time_size)])
    far_pack = pl.pallas_call(
        touch_kernel,
        out_shape=jax.ShapeDtypeStruct((pack_rows, LANE), bf16),
        in_specs=[VMEM, HBM],
        out_specs=VMEM,
        compiler_params=PARAMS,
        cost_estimate=pl.CostEstimate(flops=10**6, bytes_accessed=400000, transcendentals=0),
        name="touch",
    )(pack, both)
    far = moved(far_pack, -3, 3)
    swapped = moved(side, 1, -1)

    odd = (domain % 2)[None]
    side_later = side
    part = pl.pallas_call(
        near_kernel,
        out_shape=jax.ShapeDtypeStruct((rows, length), jnp.float32),
        in_specs=[SMEM] + [VMEM] * 3,
        out_specs=VMEM,
        compiler_params=PARAMS,
        cost_estimate=pl.CostEstimate(flops=10**10, bytes_accessed=1000000, transcendentals=0),
        name="near",
    )(odd, partners.T, both, side_later)
    sums = pl.pallas_call(
        sums_kernel,
        out_shape=jax.ShapeDtypeStruct((LAGS // LANE, 4, LANE), jnp.float32),
        in_specs=[SMEM] + [VMEM] * 6,
        out_specs=VMEM,
        scratch_shapes=[pltpu.VMEM((rows, length), bf16)],
        compiler_params=PARAMS,
        cost_estimate=pl.CostEstimate(flops=2 * 300000000, bytes_accessed=2500000, transcendentals=0),
        name="sums",
    )(odd, partners.T, part, far, swapped, own, following)

    shares = lax.all_to_all(sums, "tm", 0, 0)
    lag_share = LAGS // time_size
    lag_index = lax.axis_index("tm") * lag_share + jnp.arange(lag_share, dtype=jnp.int32)
    anchor_count = (length * time_size - lag_index).astype(jnp.float32)
    return (jnp.sum(shares, axis=0) / anchor_count[None, :])[None]


def solution(mesh):
    return jax.shard_map(
        per_device,
        mesh=mesh,
        in_specs=(
            P("space", None, "tm"),
            P("space", None, "tm"),
            P("space", None),
            P("space", None, None),
            P("space", None),
        ),
        out_specs=P("space", None, "tm"),
        check_vma=False,
    )
```

```python
import jax
import jax.numpy as jnp
from jax import lax
from jax.experimental import pallas as pl
from jax.experimental.pallas import tpu as pltpu
from jax.sharding import PartitionSpec as P

BLK = 2
LAGS = 1024
REACH = 3
BLOCKS = 32
LANE = 128
TILE = 128
VMEM_BYTES = 32 * 1024 * 1024


def pair_sums(rates):
    molecules = rates.shape[0]
    row = lax.broadcasted_iota(jnp.int32, (molecules // BLK, molecules), 0)
    col = lax.broadcasted_iota(jnp.int32, (molecules // BLK, molecules), 1)
    ones = ((col >= row * BLK) & (col < row * BLK + BLK)).astype(jnp.bfloat16)
    return jnp.dot(ones, rates, preferred_element_type=jnp.float32).astype(jnp.bfloat16)


def totals_kernel(dipole_hbm, polar_hbm, own_ref, dipole_ref, polar_ref, sem):
    components, molecules, length = dipole_ref.shape
    blocks = molecules // BLK
    copies = [
        pltpu.make_async_copy(dipole_hbm, dipole_ref, sem.at[0]),
        pltpu.make_async_copy(polar_hbm, polar_ref, sem.at[1]),
    ]
    for copy in copies:
        copy.start()
    for number, (copy, ref) in enumerate(zip(copies, (dipole_ref, polar_ref))):
        copy.wait()
        for c in range(components):
            at = (number * components + c) * blocks
            own_ref[at : at + blocks, :] = pair_sums(ref[c])


def pack_kernel(domain_ref, own_ref, counts_ref, lists_ref, pack_ref):
    rows, length = own_ref.shape
    for j in range(length // LANE):
        pack_ref[j * rows : (j + 1) * rows, :] = own_ref[:, j * LANE : (j + 1) * LANE]
    capacity, domains = lists_ref.shape
    slot = lax.broadcasted_iota(jnp.int32, (16, domains), 0)
    offset = jnp.where(slot < REACH, slot - REACH, slot - REACH + 1)
    target = lax.rem(domain_ref[0] + offset + domains, domains)
    hot = (lax.broadcasted_iota(jnp.int32, (16, domains), 1) == target) & (slot < 2 * REACH)
    picked = lax.dot_general(
        hot.astype(jnp.bfloat16),
        lists_ref[...].astype(jnp.float32).astype(jnp.bfloat16),
        (((1,), (1,)), ((), ())),
        preferred_element_type=jnp.float32,
    )
    count = jnp.sum(jnp.where(hot, counts_ref[...], 0).astype(jnp.float32), axis=1, keepdims=True)
    entry = lax.broadcasted_iota(jnp.int32, (16, capacity), 1).astype(jnp.float32)
    meta = jnp.where(entry < count, picked, -1.0)
    meta = jnp.concatenate([meta, jnp.full((16, LANE - capacity), -1.0, jnp.float32)], axis=1)
    base = rows * (length // LANE)
    pack_ref[base : base + 16, :] = meta.astype(jnp.bfloat16)


def select_kernel(odd_ref, pack_ref, unused_ref, far_ref):
    blocks = BLOCKS
    rows = 3 * blocks
    tiles = (pack_ref.shape[0] - 16) // rows
    slot_row = lax.broadcasted_iota(jnp.int32, (16, LANE), 0)
    meta = pack_ref[rows * tiles : rows * tiles + 16, :].astype(jnp.float32)
    slot = jnp.where(odd_ref[0] == 1, 2 * REACH - 1, 0)
    listed = jnp.sum(jnp.where(slot_row == slot, meta, 0.0), axis=0, keepdims=True)
    number = lax.broadcasted_iota(jnp.int32, (blocks, blocks), 0).astype(jnp.float32)
    select = (listed[:, :blocks] == number).astype(jnp.bfloat16)
    capacity = far_ref.shape[0] // (3 * tiles)
    for c in range(3):
        for j in range(0, tiles, 2):
            pieces = [pack_ref[jj * rows + c * blocks : jj * rows + (c + 1) * blocks, :] for jj in (j, j + 1)]
            chosen = lax.dot_general(
                select,
                jnp.concatenate(pieces, axis=1),
                (((0,), (0,)), ((), ())),
                preferred_element_type=jnp.float32,
            )
            stack = jnp.concatenate([chosen[:capacity, :LANE], chosen[:capacity, LANE:]], axis=0)
            at = (c * tiles + j) * capacity
            far_ref[at : at + 2 * capacity, :] = stack.astype(jnp.bfloat16)


def fold(gram):
    width = gram.shape[1]
    height = gram.shape[0]
    while height > LANE:
        height //= 2
        width -= height
        gram = gram[:height, :width] + gram[height:, height : height + width]
    while height > 8:
        height //= 2
        gram = gram[:height] + pltpu.roll(gram[height:], width - height, 1)
    row = lax.broadcasted_iota(jnp.int32, gram.shape, 0)
    for bit in (4, 2, 1):
        gram = jnp.where((row & bit) != 0, pltpu.roll(gram, width - bit, 1), gram)
    return jnp.sum(gram, axis=0, keepdims=True)


def weights_of(place, meta_ref, partners_ref):
    slots, blocks = partners_ref.shape
    slot_row = lax.broadcasted_iota(jnp.int32, (16, LANE), 0)
    number = lax.broadcasted_iota(jnp.int32, (blocks, blocks), 0).astype(jnp.float32)
    meta = meta_ref[...].astype(jnp.float32)
    listed = jnp.sum(jnp.where(slot_row == 2 * REACH - 1 - place, meta, 0.0), axis=0, keepdims=True)
    select = (listed[:, :blocks] == number).astype(jnp.bfloat16)
    wanted = named_by(blocks + place * slots, partners_ref).astype(jnp.bfloat16)
    return jnp.dot(select, wanted, preferred_element_type=jnp.float32).astype(jnp.bfloat16)


def named_by(first, partners_ref):
    slots, blocks = partners_ref.shape
    wanted = lax.broadcasted_iota(jnp.int32, (blocks, blocks), 0) + first
    total = jnp.zeros((blocks, blocks), jnp.float32)
    for s in range(slots):
        total = total + jnp.where(partners_ref[s : s + 1, :] == wanted, 1.0, 0.0)
    return total


def field_terms(weight, sources, blocks, length, store):
    rows = 3 * blocks
    for c in range(3):
        for j in range(0, length // LANE, 2):
            parts = []
            for jj in (j, j + 1):
                at = jj * rows + c * blocks
                parts.append(jnp.concatenate([ref[at : at + blocks, :] for ref in sources], axis=0))
            table = jnp.concatenate(parts, axis=1)
            field = lax.dot_general(
                weight, table, (((0,), (0,)), ((), ())), preferred_element_type=jnp.float32
            )
            store(slice(c * blocks, (c + 1) * blocks), slice(j * LANE, (j + 2) * LANE), field)


def near_kernel(odd_ref, partners_ref, both_ref, side_ref, part_ref):
    slots, blocks = partners_ref.shape
    rows, length = part_ref.shape
    base = rows * (length // LANE)
    count = base + 16
    odd = odd_ref[0] == 1
    mine = named_by(0, partners_ref).astype(jnp.bfloat16)
    refs = [both_ref.at[pl.ds(0, count)], both_ref.at[pl.ds(count, count)]]
    refs += [side_ref.at[pl.ds(0, count)], side_ref.at[pl.ds(count, count)]]
    weights = [
        jnp.where(odd, weights_of(2, refs[0].at[pl.ds(base, 16)], partners_ref), mine),
        jnp.where(odd, mine, weights_of(3, refs[1].at[pl.ds(base, 16)], partners_ref)),
    ]
    for ref, at_even, at_odd in ((refs[2], 1, 3), (refs[3], 2, 4)):
        weights.append(weights_of(jnp.where(odd, at_odd, at_even), ref.at[pl.ds(base, 16)], partners_ref))

    def store(row, col, field):
        part_ref[row, col] = field

    field_terms(jnp.concatenate(weights, axis=0), refs, blocks, length, store)


def sums_kernel(odd_ref, partners_ref, part_ref, far_ref, swap_ref, own_ref, next_ref, out_ref, field_ref):
    slots, blocks = partners_ref.shape
    rows = 3 * blocks
    length = own_ref.shape[1]
    base = rows * (length // LANE)
    odd = odd_ref[0] == 1
    count = base + 16
    refs = [swap_ref.at[pl.ds(0, count)], swap_ref.at[pl.ds(count, count)]]
    weights = []
    for ref, at_even, at_odd in zip(refs, (4, 5), (0, 1)):
        weights.append(weights_of(jnp.where(odd, at_odd, at_even), ref.at[pl.ds(base, 16)], partners_ref))
    named = named_by(blocks + jnp.where(odd, 2 * REACH - 1, 0) * slots, partners_ref)[:slots]
    nothing = jnp.zeros_like(named)
    first = jnp.concatenate([named, nothing], axis=0).astype(jnp.bfloat16)
    second = jnp.concatenate([nothing, named], axis=0).astype(jnp.bfloat16)

    def store(row, col, field):
        at = (row.start // blocks * (length // LANE) + col.start // LANE) * slots
        listed = far_ref[at : at + 2 * slots, :]
        far = [
            lax.dot_general(weight, listed, (((0,), (0,)), ((), ())), preferred_element_type=jnp.float32)
            for weight in (first, second)
        ]
        field_ref[row, col] = (part_ref[row, col] + field + jnp.concatenate(far, axis=1)).astype(jnp.bfloat16)

    field_terms(jnp.concatenate(weights, axis=0), refs, blocks, length, store)

    span = TILE + LAGS
    steps = length // TILE

    def later(first, count, i):
        lo = i * TILE
        here = own_ref[first : first + count, lo:length]
        return jnp.concatenate([here, next_ref[first : first + count, 0 : span - (length - lo)]], axis=1)

    def gram(anchor_first, window_first, count):
        anchors = jnp.concatenate(
            [field_ref[anchor_first : anchor_first + count, i * TILE : (i + 1) * TILE] for i in range(steps)], axis=0
        )
        window = jnp.concatenate([later(window_first, count, i) for i in range(steps)], axis=0)
        return lax.dot_general(anchors, window, (((0,), (0,)), ((), ())), preferred_element_type=jnp.float32)

    for q in range(4):
        if q == 0:
            sums = fold(gram(0, 0, rows))
        else:
            sums = fold(gram(2 * blocks, rows + (q - 1) * blocks, blocks))
        for j in range(LAGS // LANE):
            out_ref[j, q : q + 1, :] = sums[:, j * LANE : (j + 1) * LANE]


VMEM = pl.BlockSpec(memory_space=pltpu.VMEM)
HBM = pl.BlockSpec(memory_space=pltpu.HBM)
SMEM = pl.BlockSpec(memory_space=pltpu.SMEM)
TOTALS_PARAMS = pltpu.CompilerParams(vmem_limit_bytes=54784 * 1024)
PARAMS = pltpu.CompilerParams(vmem_limit_bytes=VMEM_BYTES)


def per_device(dipole_rates, polar_rates, pair_counts, send_blocks, partners):
    space_size = lax.axis_size("space")
    time_size = lax.axis_size("tm")
    domain = lax.axis_index("space").astype(jnp.int32)
    molecules, components, length = dipole_rates.shape
    blocks = molecules // BLK
    rows = components * blocks
    pack_rows = rows * (length // LANE) + 16
    bf16 = jnp.bfloat16

    def moved(value, by_even, by_odd):
        pairs = [(i, (i + (by_odd if i % 2 else by_even)) % space_size) for i in range(space_size)]
        return lax.ppermute(value, "space", pairs)

    own = pl.pallas_call(
        totals_kernel,
        out_shape=jax.ShapeDtypeStruct((2 * rows, length), bf16),
        in_specs=[HBM, HBM],
        out_specs=VMEM,
        scratch_shapes=[
            pltpu.VMEM((components, molecules, length), bf16),
            pltpu.VMEM((components, molecules, length), bf16),
            pltpu.SemaphoreType.DMA((2,)),
        ],
        compiler_params=TOTALS_PARAMS,
        cost_estimate=pl.CostEstimate(flops=4 * 32 * 64 * 3072, bytes_accessed=1200000, transcendentals=0),
        name="totals",
    )(dipole_rates.transpose(1, 0, 2), polar_rates.transpose(1, 0, 2))
    pack = pl.pallas_call(
        pack_kernel,
        out_shape=jax.ShapeDtypeStruct((pack_rows, LANE), bf16),
        grid=(1,),
        in_specs=[
            SMEM,
            pl.BlockSpec((rows, length), lambda i: (0, 0)),
            pl.BlockSpec((1, space_size), lambda i: (0, 0)),
            pl.BlockSpec((send_blocks.shape[2], space_size), lambda i: (0, 0)),
        ],
        out_specs=pl.BlockSpec((pack_rows, LANE), lambda i: (0, 0)),
        compiler_params=PARAMS,
        cost_estimate=pl.CostEstimate(flops=10**6, bytes_accessed=400000, transcendentals=0),
        name="pack",
    )(domain[None], own, pair_counts, send_blocks[0].T)

    pairs = [[2 * i, 2 * i + 1] for i in range(space_size // 2)]
    both = lax.all_gather(pack, "space", axis_index_groups=pairs, tiled=True)
    own_later = own
    side = moved(both, -1, 1)
    following = lax.ppermute(own_later, "tm", [(i, i - 1) for i in range(1, time_size)])
    odd = (domain % 2)[None]
    far_pack = pl.pallas_call(
        select_kernel,
        out_shape=jax.ShapeDtypeStruct((rows // blocks * (length // LANE) * partners.shape[1], LANE), bf16),
        in_specs=[SMEM, VMEM, HBM],
        out_specs=VMEM,
        compiler_params=PARAMS,
        cost_estimate=pl.CostEstimate(flops=10**6, bytes_accessed=400000, transcendentals=0),
        name="select",
    )(odd, pack, both)
    far = moved(far_pack, -3, 3)
    swapped = moved(side, 1, -1)

    side_later = side
    part = pl.pallas_call(
        near_kernel,
        out_shape=jax.ShapeDtypeStruct((rows, length), jnp.float32),
        in_specs=[SMEM] + [VMEM] * 3,
        out_specs=VMEM,
        compiler_params=PARAMS,
        cost_estimate=pl.CostEstimate(flops=10**10, bytes_accessed=1000000, transcendentals=0),
        name="near",
    )(odd, partners.T, both, side_later)
    sums = pl.pallas_call(
        sums_kernel,
        out_shape=jax.ShapeDtypeStruct((LAGS // LANE, 4, LANE), jnp.float32),
        in_specs=[SMEM] + [VMEM] * 6,
        out_specs=VMEM,
        scratch_shapes=[pltpu.VMEM((rows, length), bf16)],
        compiler_params=PARAMS,
        cost_estimate=pl.CostEstimate(flops=2 * 300000000, bytes_accessed=2500000, transcendentals=0),
        name="sums",
    )(odd, partners.T, part, far, swapped, own, following)

    shares = lax.all_to_all(sums, "tm", 0, 0)
    lag_share = LAGS // time_size
    lag_index = lax.axis_index("tm") * lag_share + jnp.arange(lag_share, dtype=jnp.int32)
    anchor_count = (length * time_size - lag_index).astype(jnp.float32)
    return (jnp.sum(shares, axis=0) / anchor_count[None, :])[None]


def solution(mesh):
    return jax.shard_map(
        per_device,
        mesh=mesh,
        in_specs=(
            P("space", None, "tm"),
            P("space", None, "tm"),
            P("space", None),
            P("space", None, None),
            P("space", None),
        ),
        out_specs=P("space", None, "tm"),
        check_vma=False,
    )
```

```python
import functools

import jax
import jax.numpy as jnp
from jax import lax
from jax.experimental import pallas as pl
from jax.experimental.pallas import tpu as pltpu
from jax.sharding import PartitionSpec as P

BLK = 2
LAGS = 1024
REACH = 3
BLOCKS = 32
LANE = 128
TILE = 128
VMEM_BYTES = 32 * 1024 * 1024


def pair_sums(rates):
    molecules = rates.shape[0]
    row = lax.broadcasted_iota(jnp.int32, (molecules // BLK, molecules), 0)
    col = lax.broadcasted_iota(jnp.int32, (molecules // BLK, molecules), 1)
    ones = ((col >= row * BLK) & (col < row * BLK + BLK)).astype(jnp.bfloat16)
    return jnp.dot(ones, rates, preferred_element_type=jnp.float32).astype(jnp.bfloat16)


def totals_kernel(dipole_hbm, polar_hbm, own_ref, dipole_ref, polar_ref, sem):
    components, molecules, length = dipole_ref.shape
    blocks = molecules // BLK
    copies = [
        pltpu.make_async_copy(dipole_hbm, dipole_ref, sem.at[0]),
        pltpu.make_async_copy(polar_hbm, polar_ref, sem.at[1]),
    ]
    for copy in copies:
        copy.start()
    for number, (copy, ref) in enumerate(zip(copies, (dipole_ref, polar_ref))):
        copy.wait()
        for c in range(components):
            at = (number * components + c) * blocks
            own_ref[at : at + blocks, :] = pair_sums(ref[c])


def pack_kernel(domain_ref, own_ref, counts_ref, lists_ref, pack_ref):
    rows, length = own_ref.shape
    for j in range(length // LANE):
        pack_ref[j * rows : (j + 1) * rows, :] = own_ref[:, j * LANE : (j + 1) * LANE]
    capacity, domains = lists_ref.shape
    slot = lax.broadcasted_iota(jnp.int32, (16, domains), 0)
    offset = jnp.where(slot < REACH, slot - REACH, slot - REACH + 1)
    target = lax.rem(domain_ref[0] + offset + domains, domains)
    hot = (lax.broadcasted_iota(jnp.int32, (16, domains), 1) == target) & (slot < 2 * REACH)
    picked = lax.dot_general(
        hot.astype(jnp.bfloat16),
        lists_ref[...].astype(jnp.float32).astype(jnp.bfloat16),
        (((1,), (1,)), ((), ())),
        preferred_element_type=jnp.float32,
    )
    count = jnp.sum(jnp.where(hot, counts_ref[...], 0).astype(jnp.float32), axis=1, keepdims=True)
    entry = lax.broadcasted_iota(jnp.int32, (16, capacity), 1).astype(jnp.float32)
    meta = jnp.where(entry < count, picked, -1.0)
    meta = jnp.concatenate([meta, jnp.full((16, LANE - capacity), -1.0, jnp.float32)], axis=1)
    base = rows * (length // LANE)
    pack_ref[base : base + 16, :] = meta.astype(jnp.bfloat16)


def select_kernel(odd_ref, pack_ref, unused_ref, far_ref):
    blocks = BLOCKS
    rows = 3 * blocks
    tiles = (pack_ref.shape[0] - 16) // rows
    slot_row = lax.broadcasted_iota(jnp.int32, (16, LANE), 0)
    meta = pack_ref[rows * tiles : rows * tiles + 16, :].astype(jnp.float32)
    slot = jnp.where(odd_ref[0] == 1, 2 * REACH - 1, 0)
    listed = jnp.sum(jnp.where(slot_row == slot, meta, 0.0), axis=0, keepdims=True)
    number = lax.broadcasted_iota(jnp.int32, (blocks, blocks), 0).astype(jnp.float32)
    select = (listed[:, :blocks] == number).astype(jnp.bfloat16)
    capacity = far_ref.shape[0] // (3 * tiles)
    for c in range(3):
        for j in range(0, tiles, 2):
            pieces = [pack_ref[jj * rows + c * blocks : jj * rows + (c + 1) * blocks, :] for jj in (j, j + 1)]
            chosen = lax.dot_general(
                select,
                jnp.concatenate(pieces, axis=1),
                (((0,), (0,)), ((), ())),
                preferred_element_type=jnp.float32,
            )
            stack = jnp.concatenate([chosen[:capacity, :LANE], chosen[:capacity, LANE:]], axis=0)
            at = (c * tiles + j) * capacity
            far_ref[at : at + 2 * capacity, :] = stack.astype(jnp.bfloat16)


def fold(gram):
    width = gram.shape[1]
    height = gram.shape[0]
    while height > LANE:
        height //= 2
        width -= height
        gram = gram[:height, :width] + gram[height:, height : height + width]
    while height > 8:
        height //= 2
        gram = gram[:height] + pltpu.roll(gram[height:], width - height, 1)
    row = lax.broadcasted_iota(jnp.int32, gram.shape, 0)
    for bit in (4, 2, 1):
        gram = jnp.where((row & bit) != 0, pltpu.roll(gram, width - bit, 1), gram)
    return jnp.sum(gram, axis=0, keepdims=True)


def weights_of(place, meta_ref, partners_ref):
    slots, blocks = partners_ref.shape
    slot_row = lax.broadcasted_iota(jnp.int32, (16, LANE), 0)
    number = lax.broadcasted_iota(jnp.int32, (blocks, blocks), 0).astype(jnp.float32)
    meta = meta_ref[...].astype(jnp.float32)
    listed = jnp.sum(jnp.where(slot_row == 2 * REACH - 1 - place, meta, 0.0), axis=0, keepdims=True)
    select = (listed[:, :blocks] == number).astype(jnp.bfloat16)
    wanted = named_by(blocks + place * slots, partners_ref).astype(jnp.bfloat16)
    return jnp.dot(select, wanted, preferred_element_type=jnp.float32).astype(jnp.bfloat16)


def named_by(first, partners_ref):
    slots, blocks = partners_ref.shape
    wanted = lax.broadcasted_iota(jnp.int32, (blocks, blocks), 0) + first
    total = jnp.zeros((blocks, blocks), jnp.float32)
    for s in range(slots):
        total = total + jnp.where(partners_ref[s : s + 1, :] == wanted, 1.0, 0.0)
    return total


def field_terms(weight, sources, blocks, length, store):
    rows = 3 * blocks
    for c in range(3):
        for j in range(0, length // LANE, 2):
            parts = []
            for jj in (j, j + 1):
                at = jj * rows + c * blocks
                parts.append(jnp.concatenate([ref[at : at + blocks, :] for ref in sources], axis=0))
            table = jnp.concatenate(parts, axis=1)
            field = lax.dot_general(
                weight, table, (((0,), (0,)), ((), ())), preferred_element_type=jnp.float32
            )
            store(slice(c * blocks, (c + 1) * blocks), slice(j * LANE, (j + 2) * LANE), field)


def near_kernel(odd_ref, partners_ref, both_ref, side_ref, part_ref):
    slots, blocks = partners_ref.shape
    rows, length = part_ref.shape
    base = rows * (length // LANE)
    count = base + 16
    odd = odd_ref[0] == 1
    mine = named_by(0, partners_ref).astype(jnp.bfloat16)
    refs = [both_ref.at[pl.ds(0, count)], both_ref.at[pl.ds(count, count)]]
    refs += [side_ref.at[pl.ds(0, count)], side_ref.at[pl.ds(count, count)]]
    weights = [
        jnp.where(odd, weights_of(2, refs[0].at[pl.ds(base, 16)], partners_ref), mine),
        jnp.where(odd, mine, weights_of(3, refs[1].at[pl.ds(base, 16)], partners_ref)),
    ]
    for ref, at_even, at_odd in ((refs[2], 1, 3), (refs[3], 2, 4)):
        weights.append(weights_of(jnp.where(odd, at_odd, at_even), ref.at[pl.ds(base, 16)], partners_ref))

    def store(row, col, field):
        part_ref[row, col] = field

    field_terms(jnp.concatenate(weights, axis=0), refs, blocks, length, store)


def sums_kernel(steps_in_all, odd_ref, partners_ref, part_ref, far_ref, swap_ref, own_ref, next_ref, out_ref, field_ref):
    slots, blocks = partners_ref.shape
    rows = 3 * blocks
    length = own_ref.shape[1]
    base = rows * (length // LANE)
    odd = odd_ref[0] == 1
    count = base + 16
    refs = [swap_ref.at[pl.ds(0, count)], swap_ref.at[pl.ds(count, count)]]
    weights = []
    for ref, at_even, at_odd in zip(refs, (4, 5), (0, 1)):
        weights.append(weights_of(jnp.where(odd, at_odd, at_even), ref.at[pl.ds(base, 16)], partners_ref))
    named = named_by(blocks + jnp.where(odd, 2 * REACH - 1, 0) * slots, partners_ref)[:slots]
    nothing = jnp.zeros_like(named)
    first = jnp.concatenate([named, nothing], axis=0).astype(jnp.bfloat16)
    second = jnp.concatenate([nothing, named], axis=0).astype(jnp.bfloat16)

    def store(row, col, field):
        at = (row.start // blocks * (length // LANE) + col.start // LANE) * slots
        listed = far_ref[at : at + 2 * slots, :]
        far = [
            lax.dot_general(weight, listed, (((0,), (0,)), ((), ())), preferred_element_type=jnp.float32)
            for weight in (first, second)
        ]
        field_ref[row, col] = (part_ref[row, col] + field + jnp.concatenate(far, axis=1)).astype(jnp.bfloat16)

    field_terms(jnp.concatenate(weights, axis=0), refs, blocks, length, store)

    span = TILE + LAGS
    steps = length // TILE

    def later(first, count, i):
        lo = i * TILE
        here = own_ref[first : first + count, lo:length]
        return jnp.concatenate([here, next_ref[first : first + count, 0 : span - (length - lo)]], axis=1)

    def gram(anchor_first, window_first, count):
        anchors = jnp.concatenate(
            [field_ref[anchor_first : anchor_first + count, i * TILE : (i + 1) * TILE] for i in range(steps)], axis=0
        )
        window = jnp.concatenate([later(window_first, count, i) for i in range(steps)], axis=0)
        return lax.dot_general(anchors, window, (((0,), (0,)), ((), ())), preferred_element_type=jnp.float32)

    for q in range(4):
        if q == 0:
            sums = fold(gram(0, 0, rows))
        else:
            sums = fold(gram(2 * blocks, rows + (q - 1) * blocks, blocks))
        for j in range(LAGS // LANE):
            lag = lax.broadcasted_iota(jnp.int32, (1, LANE), 1) + j * LANE
            anchors = (steps_in_all - lag).astype(jnp.float32)
            out_ref[j, q : q + 1, :] = sums[:, j * LANE : (j + 1) * LANE] / anchors


VMEM = pl.BlockSpec(memory_space=pltpu.VMEM)
HBM = pl.BlockSpec(memory_space=pltpu.HBM)
SMEM = pl.BlockSpec(memory_space=pltpu.SMEM)
TOTALS_PARAMS = pltpu.CompilerParams(vmem_limit_bytes=54784 * 1024)
PARAMS = pltpu.CompilerParams(vmem_limit_bytes=VMEM_BYTES)


def per_device(dipole_rates, polar_rates, pair_counts, send_blocks, partners):
    space_size = lax.axis_size("space")
    time_size = lax.axis_size("tm")
    domain = lax.axis_index("space").astype(jnp.int32)
    molecules, components, length = dipole_rates.shape
    blocks = molecules // BLK
    rows = components * blocks
    pack_rows = rows * (length // LANE) + 16
    bf16 = jnp.bfloat16

    def moved(value, by_even, by_odd):
        pairs = [(i, (i + (by_odd if i % 2 else by_even)) % space_size) for i in range(space_size)]
        return lax.ppermute(value, "space", pairs)

    own = pl.pallas_call(
        totals_kernel,
        out_shape=jax.ShapeDtypeStruct((2 * rows, length), bf16),
        in_specs=[HBM, HBM],
        out_specs=VMEM,
        scratch_shapes=[
            pltpu.VMEM((components, molecules, length), bf16),
            pltpu.VMEM((components, molecules, length), bf16),
            pltpu.SemaphoreType.DMA((2,)),
        ],
        compiler_params=TOTALS_PARAMS,
        cost_estimate=pl.CostEstimate(flops=4 * 32 * 64 * 3072, bytes_accessed=1200000, transcendentals=0),
        name="totals",
    )(dipole_rates.transpose(1, 0, 2), polar_rates.transpose(1, 0, 2))
    pack = pl.pallas_call(
        pack_kernel,
        out_shape=jax.ShapeDtypeStruct((pack_rows, LANE), bf16),
        grid=(1,),
        in_specs=[
            SMEM,
            pl.BlockSpec((rows, length), lambda i: (0, 0)),
            pl.BlockSpec((1, space_size), lambda i: (0, 0)),
            pl.BlockSpec((send_blocks.shape[2], space_size), lambda i: (0, 0)),
        ],
        out_specs=pl.BlockSpec((pack_rows, LANE), lambda i: (0, 0)),
        compiler_params=PARAMS,
        cost_estimate=pl.CostEstimate(flops=10**6, bytes_accessed=400000, transcendentals=0),
        name="pack",
    )(domain[None], own, pair_counts, send_blocks[0].T)

    pairs = [[2 * i, 2 * i + 1] for i in range(space_size // 2)]
    both = lax.all_gather(pack, "space", axis_index_groups=pairs, tiled=True)
    own_later = own
    side = moved(both, -1, 1)
    following = lax.ppermute(own_later, "tm", [(i, i - 1) for i in range(1, time_size)])
    odd = (domain % 2)[None]
    far_pack = pl.pallas_call(
        select_kernel,
        out_shape=jax.ShapeDtypeStruct((rows // blocks * (length // LANE) * partners.shape[1], LANE), bf16),
        in_specs=[SMEM, VMEM, HBM],
        out_specs=VMEM,
        compiler_params=PARAMS,
        cost_estimate=pl.CostEstimate(flops=10**6, bytes_accessed=400000, transcendentals=0),
        name="select",
    )(odd, pack, both)
    far = moved(far_pack, -3, 3)
    swapped = moved(side, 1, -1)

    side_later = side
    part = pl.pallas_call(
        near_kernel,
        out_shape=jax.ShapeDtypeStruct((rows, length), jnp.float32),
        in_specs=[SMEM] + [VMEM] * 3,
        out_specs=VMEM,
        compiler_params=PARAMS,
        cost_estimate=pl.CostEstimate(flops=10**10, bytes_accessed=1000000, transcendentals=0),
        name="near",
    )(odd, partners.T, both, side_later)
    sums = pl.pallas_call(
        functools.partial(sums_kernel, length * time_size),
        out_shape=jax.ShapeDtypeStruct((LAGS // LANE, 4, LANE), jnp.float32),
        in_specs=[SMEM] + [VMEM] * 6,
        out_specs=VMEM,
        scratch_shapes=[pltpu.VMEM((rows, length), bf16)],
        compiler_params=PARAMS,
        cost_estimate=pl.CostEstimate(flops=2 * 300000000, bytes_accessed=2500000, transcendentals=0),
        name="sums",
    )(odd, partners.T, part, far, swapped, own, following)

    shares = lax.all_to_all(sums, "tm", 0, 0)
    return jnp.sum(shares, axis=0)[None]


def solution(mesh):
    return jax.shard_map(
        per_device,
        mesh=mesh,
        in_specs=(
            P("space", None, "tm"),
            P("space", None, "tm"),
            P("space", None),
            P("space", None, None),
            P("space", None),
        ),
        out_specs=P("space", None, "tm"),
        check_vma=False,
    )
```

```python
import functools

import jax
import jax.numpy as jnp
from jax import lax
from jax.experimental import pallas as pl
from jax.experimental.pallas import tpu as pltpu
from jax.sharding import PartitionSpec as P

BLK = 2
LAGS = 1024
REACH = 3
BLOCKS = 32
LANE = 128
TILE = 128
VMEM_BYTES = 32 * 1024 * 1024


def pair_sums(rates):
    molecules = rates.shape[0]
    row = lax.broadcasted_iota(jnp.int32, (molecules // BLK, molecules), 0)
    col = lax.broadcasted_iota(jnp.int32, (molecules // BLK, molecules), 1)
    ones = ((col >= row * BLK) & (col < row * BLK + BLK)).astype(jnp.bfloat16)
    return jnp.dot(ones, rates, preferred_element_type=jnp.float32).astype(jnp.bfloat16)


def totals_kernel(dipole_hbm, polar_hbm, own_ref, dipole_ref, polar_ref, sem):
    components, molecules, length = dipole_ref.shape
    blocks = molecules // BLK
    copies = [
        pltpu.make_async_copy(dipole_hbm, dipole_ref, sem.at[0]),
        pltpu.make_async_copy(polar_hbm, polar_ref, sem.at[1]),
    ]
    for copy in copies:
        copy.start()
    for number, (copy, ref) in enumerate(zip(copies, (dipole_ref, polar_ref))):
        copy.wait()
        for c in range(components):
            at = (number * components + c) * blocks
            own_ref[at : at + blocks, :] = pair_sums(ref[c])


def pack_kernel(domain_ref, own_ref, counts_ref, lists_ref, pack_ref):
    rows, length = own_ref.shape
    for j in range(length // LANE):
        pack_ref[j * rows : (j + 1) * rows, :] = own_ref[:, j * LANE : (j + 1) * LANE]
    capacity, domains = lists_ref.shape
    slot = lax.broadcasted_iota(jnp.int32, (16, domains), 0)
    offset = jnp.where(slot < REACH, slot - REACH, slot - REACH + 1)
    target = lax.rem(domain_ref[0] + offset + domains, domains)
    hot = (lax.broadcasted_iota(jnp.int32, (16, domains), 1) == target) & (slot < 2 * REACH)
    picked = lax.dot_general(
        hot.astype(jnp.bfloat16),
        lists_ref[...].astype(jnp.float32).astype(jnp.bfloat16),
        (((1,), (1,)), ((), ())),
        preferred_element_type=jnp.float32,
    )
    count = jnp.sum(jnp.where(hot, counts_ref[...], 0).astype(jnp.float32), axis=1, keepdims=True)
    entry = lax.broadcasted_iota(jnp.int32, (16, capacity), 1).astype(jnp.float32)
    meta = jnp.where(entry < count, picked, -1.0)
    meta = jnp.concatenate([meta, jnp.full((16, LANE - capacity), -1.0, jnp.float32)], axis=1)
    base = rows * (length // LANE)
    pack_ref[base : base + 16, :] = meta.astype(jnp.bfloat16)


def select_kernel(odd_ref, pack_ref, unused_ref, far_ref):
    blocks = BLOCKS
    rows = 3 * blocks
    tiles = (pack_ref.shape[0] - 16) // rows
    slot_row = lax.broadcasted_iota(jnp.int32, (16, LANE), 0)
    meta = pack_ref[rows * tiles : rows * tiles + 16, :].astype(jnp.float32)
    slot = jnp.where(odd_ref[0] == 1, 2 * REACH - 1, 0)
    listed = jnp.sum(jnp.where(slot_row == slot, meta, 0.0), axis=0, keepdims=True)
    number = lax.broadcasted_iota(jnp.int32, (blocks, blocks), 0).astype(jnp.float32)
    select = (listed[:, :blocks] == number).astype(jnp.bfloat16)
    capacity = far_ref.shape[0] // (3 * tiles)
    for c in range(3):
        for j in range(0, tiles, 2):
            pieces = [pack_ref[jj * rows + c * blocks : jj * rows + (c + 1) * blocks, :] for jj in (j, j + 1)]
            chosen = lax.dot_general(
                select,
                jnp.concatenate(pieces, axis=1),
                (((0,), (0,)), ((), ())),
                preferred_element_type=jnp.float32,
            )
            stack = jnp.concatenate([chosen[:capacity, :LANE], chosen[:capacity, LANE:]], axis=0)
            at = (c * tiles + j) * capacity
            far_ref[at : at + 2 * capacity, :] = stack.astype(jnp.bfloat16)


def fold(gram):
    width = gram.shape[1]
    height = gram.shape[0]
    while height > LANE:
        height //= 2
        width -= height
        gram = gram[:height, :width] + gram[height:, height : height + width]
    while height > 8:
        height //= 2
        gram = gram[:height] + pltpu.roll(gram[height:], width - height, 1)
    row = lax.broadcasted_iota(jnp.int32, gram.shape, 0)
    for bit in (4, 2, 1):
        gram = jnp.where((row & bit) != 0, pltpu.roll(gram, width - bit, 1), gram)
    return jnp.sum(gram, axis=0, keepdims=True)


def weights_of(place, meta_ref, partners_ref):
    slots, blocks = partners_ref.shape
    slot_row = lax.broadcasted_iota(jnp.int32, (16, LANE), 0)
    number = lax.broadcasted_iota(jnp.int32, (blocks, blocks), 0).astype(jnp.float32)
    meta = meta_ref[...].astype(jnp.float32)
    listed = jnp.sum(jnp.where(slot_row == 2 * REACH - 1 - place, meta, 0.0), axis=0, keepdims=True)
    select = (listed[:, :blocks] == number).astype(jnp.bfloat16)
    wanted = named_by(blocks + place * slots, partners_ref).astype(jnp.bfloat16)
    return jnp.dot(select, wanted, preferred_element_type=jnp.float32).astype(jnp.bfloat16)


def named_by(first, partners_ref):
    slots, blocks = partners_ref.shape
    wanted = lax.broadcasted_iota(jnp.int32, (blocks, blocks), 0) + first
    total = jnp.zeros((blocks, blocks), jnp.float32)
    for s in range(slots):
        total = total + jnp.where(partners_ref[s : s + 1, :] == wanted, 1.0, 0.0)
    return total


def field_terms(weight, sources, blocks, length, store):
    rows = 3 * blocks
    for c in range(3):
        for j in range(0, length // LANE, 2):
            parts = []
            for jj in (j, j + 1):
                at = jj * rows + c * blocks
                parts.append(jnp.concatenate([ref[at : at + blocks, :] for ref in sources], axis=0))
            table = jnp.concatenate(parts, axis=1)
            field = lax.dot_general(
                weight, table, (((0,), (0,)), ((), ())), preferred_element_type=jnp.float32
            )
            store(slice(c * blocks, (c + 1) * blocks), slice(j * LANE, (j + 2) * LANE), field)


def near_kernel(odd_ref, partners_ref, both_ref, side_ref, part_ref):
    slots, blocks = partners_ref.shape
    rows, length = part_ref.shape
    base = rows * (length // LANE)
    count = base + 16
    odd = odd_ref[0] == 1
    mine = named_by(0, partners_ref).astype(jnp.bfloat16)
    refs = [both_ref.at[pl.ds(0, count)], both_ref.at[pl.ds(count, count)]]
    refs += [side_ref.at[pl.ds(0, count)], side_ref.at[pl.ds(count, count)]]
    weights = [
        jnp.where(odd, weights_of(2, refs[0].at[pl.ds(base, 16)], partners_ref), mine),
        jnp.where(odd, mine, weights_of(3, refs[1].at[pl.ds(base, 16)], partners_ref)),
    ]
    for ref, at_even, at_odd in ((refs[2], 1, 3), (refs[3], 2, 4)):
        weights.append(weights_of(jnp.where(odd, at_odd, at_even), ref.at[pl.ds(base, 16)], partners_ref))

    def store(row, col, field):
        part_ref[row, col] = field

    field_terms(jnp.concatenate(weights, axis=0), refs, blocks, length, store)


def sums_kernel(steps_in_all, odd_ref, partners_ref, part_ref, far_ref, swap_ref, own_ref, next_ref, out_ref, field_ref):
    slots, blocks = partners_ref.shape
    rows = 3 * blocks
    length = own_ref.shape[1]
    base = rows * (length // LANE)
    odd = odd_ref[0] == 1
    count = base + 16
    refs = [swap_ref.at[pl.ds(0, count)], swap_ref.at[pl.ds(count, count)]]
    weights = []
    for ref, at_even, at_odd in zip(refs, (4, 5), (0, 1)):
        weights.append(weights_of(jnp.where(odd, at_odd, at_even), ref.at[pl.ds(base, 16)], partners_ref))
    named = named_by(blocks + jnp.where(odd, 2 * REACH - 1, 0) * slots, partners_ref)[:slots]
    nothing = jnp.zeros_like(named)
    first = jnp.concatenate([named, nothing], axis=0).astype(jnp.bfloat16)
    second = jnp.concatenate([nothing, named], axis=0).astype(jnp.bfloat16)

    def store(row, col, field):
        at = (row.start // blocks * (length // LANE) + col.start // LANE) * slots
        listed = far_ref[at : at + 2 * slots, :]
        far = [
            lax.dot_general(weight, listed, (((0,), (0,)), ((), ())), preferred_element_type=jnp.float32)
            for weight in (first, second)
        ]
        field_ref[row, col] = (part_ref[row, col] + field + jnp.concatenate(far, axis=1)).astype(jnp.bfloat16)

    field_terms(jnp.concatenate(weights, axis=0), refs, blocks, length, store)

    def later(first, count, i, tile):
        lo = i * tile
        span = tile + LAGS
        here = own_ref[first : first + count, lo:length]
        return jnp.concatenate([here, next_ref[first : first + count, 0 : span - (length - lo)]], axis=1)

    def gram(anchor_first, window_first, count, tile):
        steps = length // tile
        anchors = jnp.concatenate(
            [field_ref[anchor_first : anchor_first + count, i * tile : (i + 1) * tile] for i in range(steps)], axis=0
        )
        window = jnp.concatenate([later(window_first, count, i, tile) for i in range(steps)], axis=0)
        return lax.dot_general(anchors, window, (((0,), (0,)), ((), ())), preferred_element_type=jnp.float32)

    for q in range(4):
        if q == 0:
            sums = fold(gram(0, 0, rows, 2 * TILE))
        else:
            sums = fold(gram(2 * blocks, rows + (q - 1) * blocks, blocks, TILE))
        for j in range(LAGS // LANE):
            lag = lax.broadcasted_iota(jnp.int32, (1, LANE), 1) + j * LANE
            anchors = (steps_in_all - lag).astype(jnp.float32)
            out_ref[j, q : q + 1, :] = sums[:, j * LANE : (j + 1) * LANE] / anchors


VMEM = pl.BlockSpec(memory_space=pltpu.VMEM)
HBM = pl.BlockSpec(memory_space=pltpu.HBM)
SMEM = pl.BlockSpec(memory_space=pltpu.SMEM)
TOTALS_PARAMS = pltpu.CompilerParams(vmem_limit_bytes=54784 * 1024)
PARAMS = pltpu.CompilerParams(vmem_limit_bytes=VMEM_BYTES)


def per_device(dipole_rates, polar_rates, pair_counts, send_blocks, partners):
    space_size = lax.axis_size("space")
    time_size = lax.axis_size("tm")
    domain = lax.axis_index("space").astype(jnp.int32)
    molecules, components, length = dipole_rates.shape
    blocks = molecules // BLK
    rows = components * blocks
    pack_rows = rows * (length // LANE) + 16
    bf16 = jnp.bfloat16

    def moved(value, by_even, by_odd):
        pairs = [(i, (i + (by_odd if i % 2 else by_even)) % space_size) for i in range(space_size)]
        return lax.ppermute(value, "space", pairs)

    own = pl.pallas_call(
        totals_kernel,
        out_shape=jax.ShapeDtypeStruct((2 * rows, length), bf16),
        in_specs=[HBM, HBM],
        out_specs=VMEM,
        scratch_shapes=[
            pltpu.VMEM((components, molecules, length), bf16),
            pltpu.VMEM((components, molecules, length), bf16),
            pltpu.SemaphoreType.DMA((2,)),
        ],
        compiler_params=TOTALS_PARAMS,
        cost_estimate=pl.CostEstimate(flops=4 * 32 * 64 * 3072, bytes_accessed=1200000, transcendentals=0),
        name="totals",
    )(dipole_rates.transpose(1, 0, 2), polar_rates.transpose(1, 0, 2))
    pack = pl.pallas_call(
        pack_kernel,
        out_shape=jax.ShapeDtypeStruct((pack_rows, LANE), bf16),
        grid=(1,),
        in_specs=[
            SMEM,
            pl.BlockSpec((rows, length), lambda i: (0, 0)),
            pl.BlockSpec((1, space_size), lambda i: (0, 0)),
            pl.BlockSpec((send_blocks.shape[2], space_size), lambda i: (0, 0)),
        ],
        out_specs=pl.BlockSpec((pack_rows, LANE), lambda i: (0, 0)),
        compiler_params=PARAMS,
        cost_estimate=pl.CostEstimate(flops=10**6, bytes_accessed=400000, transcendentals=0),
        name="pack",
    )(domain[None], own, pair_counts, send_blocks[0].T)

    pairs = [[2 * i, 2 * i + 1] for i in range(space_size // 2)]
    both = lax.all_gather(pack, "space", axis_index_groups=pairs, tiled=True)
    own_later = own
    side = moved(both, -1, 1)
    following = lax.ppermute(own_later, "tm", [(i, i - 1) for i in range(1, time_size)])
    odd = (domain % 2)[None]
    far_pack = pl.pallas_call(
        select_kernel,
        out_shape=jax.ShapeDtypeStruct((rows // blocks * (length // LANE) * partners.shape[1], LANE), bf16),
        in_specs=[SMEM, VMEM, HBM],
        out_specs=VMEM,
        compiler_params=PARAMS,
        cost_estimate=pl.CostEstimate(flops=10**6, bytes_accessed=400000, transcendentals=0),
        name="select",
    )(odd, pack, both)
    far = moved(far_pack, -3, 3)
    swapped = moved(side, 1, -1)

    side_later = side
    part = pl.pallas_call(
        near_kernel,
        out_shape=jax.ShapeDtypeStruct((rows, length), jnp.float32),
        in_specs=[SMEM] + [VMEM] * 3,
        out_specs=VMEM,
        compiler_params=PARAMS,
        cost_estimate=pl.CostEstimate(flops=10**10, bytes_accessed=1000000, transcendentals=0),
        name="near",
    )(odd, partners.T, both, side_later)
    sums = pl.pallas_call(
        functools.partial(sums_kernel, length * time_size),
        out_shape=jax.ShapeDtypeStruct((LAGS // LANE, 4, LANE), jnp.float32),
        in_specs=[SMEM] + [VMEM] * 6,
        out_specs=VMEM,
        scratch_shapes=[pltpu.VMEM((rows, length), bf16)],
        compiler_params=PARAMS,
        cost_estimate=pl.CostEstimate(flops=2 * 300000000, bytes_accessed=2500000, transcendentals=0),
        name="sums",
    )(odd, partners.T, part, far, swapped, own, following)

    shares = lax.all_to_all(sums, "tm", 0, 0)
    return jnp.sum(shares, axis=0)[None]


def solution(mesh):
    return jax.shard_map(
        per_device,
        mesh=mesh,
        in_specs=(
            P("space", None, "tm"),
            P("space", None, "tm"),
            P("space", None),
            P("space", None, None),
            P("space", None),
        ),
        out_specs=P("space", None, "tm"),
        check_vma=False,
    )
```

```python
import functools

import jax
import jax.numpy as jnp
from jax import lax
from jax.experimental import pallas as pl
from jax.experimental.pallas import tpu as pltpu
from jax.sharding import PartitionSpec as P

BLK = 2
LAGS = 1024
REACH = 3
BLOCKS = 32
LANE = 128
TILE = 128
VMEM_BYTES = 32 * 1024 * 1024


def pair_sums(rates):
    molecules = rates.shape[0]
    row = lax.broadcasted_iota(jnp.int32, (molecules // BLK, molecules), 0)
    col = lax.broadcasted_iota(jnp.int32, (molecules // BLK, molecules), 1)
    ones = ((col >= row * BLK) & (col < row * BLK + BLK)).astype(jnp.bfloat16)
    return jnp.dot(ones, rates, preferred_element_type=jnp.float32).astype(jnp.bfloat16)


def totals_kernel(dipole_hbm, polar_hbm, own_ref, dipole_ref, polar_ref, sem):
    components, molecules, length = dipole_ref.shape
    blocks = molecules // BLK
    pairs = ((dipole_hbm, dipole_ref), (polar_hbm, polar_ref))
    copies = [
        pltpu.make_async_copy(source.at[c], ref.at[c], sem.at[number * components + c])
        for number, (source, ref) in enumerate(pairs)
        for c in range(components)
    ]
    for copy in copies:
        copy.start()
    for number, (source, ref) in enumerate(pairs):
        for c in range(components):
            copies[number * components + c].wait()
            at = (number * components + c) * blocks
            own_ref[at : at + blocks, :] = pair_sums(ref[c])


def pack_kernel(domain_ref, own_ref, counts_ref, lists_ref, pack_ref):
    rows, length = own_ref.shape
    for j in range(length // LANE):
        pack_ref[j * rows : (j + 1) * rows, :] = own_ref[:, j * LANE : (j + 1) * LANE]
    capacity, domains = lists_ref.shape
    slot = lax.broadcasted_iota(jnp.int32, (16, domains), 0)
    offset = jnp.where(slot < REACH, slot - REACH, slot - REACH + 1)
    target = lax.rem(domain_ref[0] + offset + domains, domains)
    hot = (lax.broadcasted_iota(jnp.int32, (16, domains), 1) == target) & (slot < 2 * REACH)
    picked = lax.dot_general(
        hot.astype(jnp.bfloat16),
        lists_ref[...].astype(jnp.float32).astype(jnp.bfloat16),
        (((1,), (1,)), ((), ())),
        preferred_element_type=jnp.float32,
    )
    count = jnp.sum(jnp.where(hot, counts_ref[...], 0).astype(jnp.float32), axis=1, keepdims=True)
    entry = lax.broadcasted_iota(jnp.int32, (16, capacity), 1).astype(jnp.float32)
    meta = jnp.where(entry < count, picked, -1.0)
    meta = jnp.concatenate([meta, jnp.full((16, LANE - capacity), -1.0, jnp.float32)], axis=1)
    base = rows * (length // LANE)
    pack_ref[base : base + 16, :] = meta.astype(jnp.bfloat16)


def select_kernel(odd_ref, pack_ref, unused_ref, far_ref):
    blocks = BLOCKS
    rows = 3 * blocks
    tiles = (pack_ref.shape[0] - 16) // rows
    slot_row = lax.broadcasted_iota(jnp.int32, (16, LANE), 0)
    meta = pack_ref[rows * tiles : rows * tiles + 16, :].astype(jnp.float32)
    slot = jnp.where(odd_ref[0] == 1, 2 * REACH - 1, 0)
    listed = jnp.sum(jnp.where(slot_row == slot, meta, 0.0), axis=0, keepdims=True)
    number = lax.broadcasted_iota(jnp.int32, (blocks, blocks), 0).astype(jnp.float32)
    select = (listed[:, :blocks] == number).astype(jnp.bfloat16)
    capacity = far_ref.shape[0] // (3 * tiles)
    for c in range(3):
        for j in range(0, tiles, 2):
            pieces = [pack_ref[jj * rows + c * blocks : jj * rows + (c + 1) * blocks, :] for jj in (j, j + 1)]
            chosen = lax.dot_general(
                select,
                jnp.concatenate(pieces, axis=1),
                (((0,), (0,)), ((), ())),
                preferred_element_type=jnp.float32,
            )
            stack = jnp.concatenate([chosen[:capacity, :LANE], chosen[:capacity, LANE:]], axis=0)
            at = (c * tiles + j) * capacity
            far_ref[at : at + 2 * capacity, :] = stack.astype(jnp.bfloat16)


def fold(gram):
    width = gram.shape[1]
    height = gram.shape[0]
    while height > LANE:
        height //= 2
        width -= height
        gram = gram[:height, :width] + gram[height:, height : height + width]
    while height > 8:
        height //= 2
        gram = gram[:height] + pltpu.roll(gram[height:], width - height, 1)
    row = lax.broadcasted_iota(jnp.int32, gram.shape, 0)
    for bit in (4, 2, 1):
        gram = jnp.where((row & bit) != 0, pltpu.roll(gram, width - bit, 1), gram)
    return jnp.sum(gram, axis=0, keepdims=True)


def weights_of(place, meta_ref, partners_ref):
    slots, blocks = partners_ref.shape
    slot_row = lax.broadcasted_iota(jnp.int32, (16, LANE), 0)
    number = lax.broadcasted_iota(jnp.int32, (blocks, blocks), 0).astype(jnp.float32)
    meta = meta_ref[...].astype(jnp.float32)
    listed = jnp.sum(jnp.where(slot_row == 2 * REACH - 1 - place, meta, 0.0), axis=0, keepdims=True)
    select = (listed[:, :blocks] == number).astype(jnp.bfloat16)
    wanted = named_by(blocks + place * slots, partners_ref).astype(jnp.bfloat16)
    return jnp.dot(select, wanted, preferred_element_type=jnp.float32).astype(jnp.bfloat16)


def named_by(first, partners_ref):
    slots, blocks = partners_ref.shape
    wanted = lax.broadcasted_iota(jnp.int32, (blocks, blocks), 0) + first
    total = jnp.zeros((blocks, blocks), jnp.float32)
    for s in range(slots):
        total = total + jnp.where(partners_ref[s : s + 1, :] == wanted, 1.0, 0.0)
    return total


def field_terms(weight, sources, blocks, length, store):
    rows = 3 * blocks
    for c in range(3):
        for j in range(0, length // LANE, 2):
            parts = []
            for jj in (j, j + 1):
                at = jj * rows + c * blocks
                parts.append(jnp.concatenate([ref[at : at + blocks, :] for ref in sources], axis=0))
            table = jnp.concatenate(parts, axis=1)
            field = lax.dot_general(
                weight, table, (((0,), (0,)), ((), ())), preferred_element_type=jnp.float32
            )
            store(slice(c * blocks, (c + 1) * blocks), slice(j * LANE, (j + 2) * LANE), field)


def near_kernel(odd_ref, partners_ref, both_ref, side_ref, part_ref):
    slots, blocks = partners_ref.shape
    rows, length = part_ref.shape
    base = rows * (length // LANE)
    count = base + 16
    odd = odd_ref[0] == 1
    mine = named_by(0, partners_ref).astype(jnp.bfloat16)
    refs = [both_ref.at[pl.ds(0, count)], both_ref.at[pl.ds(count, count)]]
    refs += [side_ref.at[pl.ds(0, count)], side_ref.at[pl.ds(count, count)]]
    weights = [
        jnp.where(odd, weights_of(2, refs[0].at[pl.ds(base, 16)], partners_ref), mine),
        jnp.where(odd, mine, weights_of(3, refs[1].at[pl.ds(base, 16)], partners_ref)),
    ]
    for ref, at_even, at_odd in ((refs[2], 1, 3), (refs[3], 2, 4)):
        weights.append(weights_of(jnp.where(odd, at_odd, at_even), ref.at[pl.ds(base, 16)], partners_ref))

    def store(row, col, field):
        part_ref[row, col] = field

    field_terms(jnp.concatenate(weights, axis=0), refs, blocks, length, store)


def sums_kernel(steps_in_all, odd_ref, partners_ref, part_ref, far_ref, swap_ref, own_ref, next_ref, out_ref, field_ref):
    slots, blocks = partners_ref.shape
    rows = 3 * blocks
    length = own_ref.shape[1]
    base = rows * (length // LANE)
    odd = odd_ref[0] == 1
    count = base + 16
    refs = [swap_ref.at[pl.ds(0, count)], swap_ref.at[pl.ds(count, count)]]
    weights = []
    for ref, at_even, at_odd in zip(refs, (4, 5), (0, 1)):
        weights.append(weights_of(jnp.where(odd, at_odd, at_even), ref.at[pl.ds(base, 16)], partners_ref))
    named = named_by(blocks + jnp.where(odd, 2 * REACH - 1, 0) * slots, partners_ref)[:slots]
    nothing = jnp.zeros_like(named)
    first = jnp.concatenate([named, nothing], axis=0).astype(jnp.bfloat16)
    second = jnp.concatenate([nothing, named], axis=0).astype(jnp.bfloat16)

    def store(row, col, field):
        at = (row.start // blocks * (length // LANE) + col.start // LANE) * slots
        listed = far_ref[at : at + 2 * slots, :]
        far = [
            lax.dot_general(weight, listed, (((0,), (0,)), ((), ())), preferred_element_type=jnp.float32)
            for weight in (first, second)
        ]
        field_ref[row, col] = (part_ref[row, col] + field + jnp.concatenate(far, axis=1)).astype(jnp.bfloat16)

    field_terms(jnp.concatenate(weights, axis=0), refs, blocks, length, store)

    def later(first, count, i, tile):
        lo = i * tile
        span = tile + LAGS
        here = own_ref[first : first + count, lo:length]
        return jnp.concatenate([here, next_ref[first : first + count, 0 : span - (length - lo)]], axis=1)

    def gram(anchor_first, window_first, count, tile):
        steps = length // tile
        anchors = jnp.concatenate(
            [field_ref[anchor_first : anchor_first + count, i * tile : (i + 1) * tile] for i in range(steps)], axis=0
        )
        window = jnp.concatenate([later(window_first, count, i, tile) for i in range(steps)], axis=0)
        return lax.dot_general(anchors, window, (((0,), (0,)), ((), ())), preferred_element_type=jnp.float32)

    for q in range(4):
        if q == 0:
            sums = fold(gram(0, 0, rows, 2 * TILE))
        else:
            sums = fold(gram(2 * blocks, rows + (q - 1) * blocks, blocks, TILE))
        for j in range(LAGS // LANE):
            lag = lax.broadcasted_iota(jnp.int32, (1, LANE), 1) + j * LANE
            anchors = (steps_in_all - lag).astype(jnp.float32)
            out_ref[j, q : q + 1, :] = sums[:, j * LANE : (j + 1) * LANE] / anchors


VMEM = pl.BlockSpec(memory_space=pltpu.VMEM)
HBM = pl.BlockSpec(memory_space=pltpu.HBM)
SMEM = pl.BlockSpec(memory_space=pltpu.SMEM)
TOTALS_PARAMS = pltpu.CompilerParams(vmem_limit_bytes=54784 * 1024)
PARAMS = pltpu.CompilerParams(vmem_limit_bytes=VMEM_BYTES)


def per_device(dipole_rates, polar_rates, pair_counts, send_blocks, partners):
    space_size = lax.axis_size("space")
    time_size = lax.axis_size("tm")
    domain = lax.axis_index("space").astype(jnp.int32)
    molecules, components, length = dipole_rates.shape
    blocks = molecules // BLK
    rows = components * blocks
    pack_rows = rows * (length // LANE) + 16
    bf16 = jnp.bfloat16

    def moved(value, by_even, by_odd):
        pairs = [(i, (i + (by_odd if i % 2 else by_even)) % space_size) for i in range(space_size)]
        return lax.ppermute(value, "space", pairs)

    own = pl.pallas_call(
        totals_kernel,
        out_shape=jax.ShapeDtypeStruct((2 * rows, length), bf16),
        in_specs=[HBM, HBM],
        out_specs=VMEM,
        scratch_shapes=[
            pltpu.VMEM((components, molecules, length), bf16),
            pltpu.VMEM((components, molecules, length), bf16),
            pltpu.SemaphoreType.DMA((2 * components,)),
        ],
        compiler_params=TOTALS_PARAMS,
        cost_estimate=pl.CostEstimate(flops=4 * 32 * 64 * 3072, bytes_accessed=1200000, transcendentals=0),
        name="totals",
    )(dipole_rates.transpose(1, 0, 2), polar_rates.transpose(1, 0, 2))
    pack = pl.pallas_call(
        pack_kernel,
        out_shape=jax.ShapeDtypeStruct((pack_rows, LANE), bf16),
        grid=(1,),
        in_specs=[
            SMEM,
            pl.BlockSpec((rows, length), lambda i: (0, 0)),
            pl.BlockSpec((1, space_size), lambda i: (0, 0)),
            pl.BlockSpec((send_blocks.shape[2], space_size), lambda i: (0, 0)),
        ],
        out_specs=pl.BlockSpec((pack_rows, LANE), lambda i: (0, 0)),
        compiler_params=PARAMS,
        cost_estimate=pl.CostEstimate(flops=10**6, bytes_accessed=400000, transcendentals=0),
        name="pack",
    )(domain[None], own, pair_counts, send_blocks[0].T)

    pairs = [[2 * i, 2 * i + 1] for i in range(space_size // 2)]
    both = lax.all_gather(pack, "space", axis_index_groups=pairs, tiled=True)
    own_later = own
    side = moved(both, -1, 1)
    following = lax.ppermute(own_later, "tm", [(i, i - 1) for i in range(1, time_size)])
    odd = (domain % 2)[None]
    far_pack = pl.pallas_call(
        select_kernel,
        out_shape=jax.ShapeDtypeStruct((rows // blocks * (length // LANE) * partners.shape[1], LANE), bf16),
        in_specs=[SMEM, VMEM, HBM],
        out_specs=VMEM,
        compiler_params=PARAMS,
        cost_estimate=pl.CostEstimate(flops=10**6, bytes_accessed=400000, transcendentals=0),
        name="select",
    )(odd, pack, both)
    far = moved(far_pack, -3, 3)
    swapped = moved(side, 1, -1)

    side_later = side
    part = pl.pallas_call(
        near_kernel,
        out_shape=jax.ShapeDtypeStruct((rows, length), jnp.float32),
        in_specs=[SMEM] + [VMEM] * 3,
        out_specs=VMEM,
        compiler_params=PARAMS,
        cost_estimate=pl.CostEstimate(flops=10**10, bytes_accessed=1000000, transcendentals=0),
        name="near",
    )(odd, partners.T, both, side_later)
    sums = pl.pallas_call(
        functools.partial(sums_kernel, length * time_size),
        out_shape=jax.ShapeDtypeStruct((LAGS // LANE, 4, LANE), jnp.float32),
        in_specs=[SMEM] + [VMEM] * 6,
        out_specs=VMEM,
        scratch_shapes=[pltpu.VMEM((rows, length), bf16)],
        compiler_params=PARAMS,
        cost_estimate=pl.CostEstimate(flops=2 * 300000000, bytes_accessed=2500000, transcendentals=0),
        name="sums",
    )(odd, partners.T, part, far, swapped, own, following)

    shares = lax.all_to_all(sums, "tm", 0, 0)
    return jnp.sum(shares, axis=0)[None]


def solution(mesh):
    return jax.shard_map(
        per_device,
        mesh=mesh,
        in_specs=(
            P("space", None, "tm"),
            P("space", None, "tm"),
            P("space", None),
            P("space", None, None),
            P("space", None),
        ),
        out_specs=P("space", None, "tm"),
        check_vma=False,
    )
```
